32 devices in a mesh: row: 4 (over y, x), col: 8 (over z, core).
Axes of the slice: x: 2, y: 2, z: 4, core: 2. Of those that a mesh axis runs over, the one named last changes fastest.
Arguments:
- patterns: float32 [8, 16, 256, 256], P('row', 'col'), may hold values from 0.05 to 4
- background: float32 [256, 256], replicated, may hold values from 0.05 to 0.6
- offsets: int32 [8, 16, 2], P('row', 'col'), may hold values from 0 to 64
- probe_wave: float32 [2, 256, 256], replicated, may hold values from -21 to 21
- object_field: float32 [2, 512, 1024], P(None, 'row', 'col'), may hold values from -15 to 15
Outputs:
- new_object: float32 [2, 512, 1024], P(None, 'row', 'col')
- new_probe: float32 [2, 256, 256], replicated
The draws below stay inside these ranges and needn't reach their ends.
All inputs are finite; a program needn't handle non-finite values.
Results may differ from the reference program's by a relative error of at most 0.0085.
The reference program's roundings to bfloat16 on the way count: a program that leaves them out, or rounds other values in their place, can miss the bound.
Values sent between devices are 32-bit elements; how exact they have to be, the bound alone decides.
A program may use at most 64 MiB of HBM per device.

```python
import math
import jax
import jax.numpy as jnp
from jax import lax

K = 256
STEP = 64
ITERS = 2
SR = 8
SC = 16
NR = 512
NC = 1024


def draw_probe_wave(key, part):
    keys = jax.random.split(jax.random.fold_in(key, 17), 3)
    positions = jnp.arange(K, dtype=jnp.float32) / K
    ramp_up = jnp.exp(jnp.log(3.0) * positions)
    base_draw = jnp.clip(jax.random.normal(keys[0], (2, K, K), jnp.float32), -4.0, 4.0)
    factor_width = 0.8
    row_factor = ramp_up * jnp.exp(factor_width * jax.random.uniform(keys[1], (K,), jnp.float32, -1.0, 1.0))
    col_factor = jnp.exp(factor_width * jax.random.uniform(keys[2], (K,), jnp.float32, -1.0, 1.0))
    return 0.35 * base_draw * row_factor[None, :, None] * col_factor[None, None, :]


def draw_object_field(key, part):
    keys = jax.random.split(jax.random.fold_in(key, 23), 1)
    row_places = jnp.arange(NR, dtype=jnp.float32) / NR
    row_ramp = 0.4 * jnp.exp(jnp.float32(math.log(9.0)) * row_places)
    base_draw = jnp.clip(jax.random.normal(keys[0], (2, NR, NC), jnp.float32), -4.0, 4.0)
    return base_draw * row_ramp[None, :, None]


def plant(drawn, key, least, largest):
    longest = drawn.shape.index(max(drawn.shape))
    spots = []
    for shift in (0, 1):
        where = [jax.random.randint(jax.random.fold_in(key, axis), (), 0, length) for axis, length in enumerate(drawn.shape)]
        where[longest] = (where[longest] + shift) % drawn.shape[longest]
        spots.append(tuple(where))
    return drawn.at[spots[0]].set(least).at[spots[1]].set(largest)


def steps_of(own_key, dims, pieces, least, top_value):
    level, own = 1.0, jax.random.fold_in(own_key, 6)
    for dim, parts in pieces:
        heights = jnp.exp(jax.random.uniform(jax.random.fold_in(own, dim), (parts,), jnp.float32, least / len(pieces), top_value / len(pieces)))
        level = level * jnp.repeat(heights, dims[dim] // parts).reshape([-1 if axis == dim else 1 for axis in range(len(dims))])
    return level


def setup_inputs(seed: int = 0) -> dict:
    arg_keys = jax.random.split(jax.random.key(seed), 6)
    patterns = jnp.clip(jnp.exp(math.log(4.0) - 4.3820266 * jax.random.uniform(arg_keys[0], (SR, SC, K, K), jnp.float32) ** steps_of(arg_keys[0], (SR, SC, K, K), ((0, 4), (1, 8)), -0.2, 0.2)), 0.05, 4.0)
    background = jnp.clip(jax.random.uniform(arg_keys[1], (K, K), jnp.float32, 0.05, 0.6), 0.05, 0.6)
    offsets = plant(jax.random.randint(arg_keys[2], (SR, SC, 2), 0, STEP + 1), jax.random.fold_in(arg_keys[2], 1), 0, STEP).astype(jnp.int32)
    probe_wave = draw_probe_wave(jax.random.fold_in(arg_keys[5], 71), 0)
    object_field = draw_object_field(jax.random.fold_in(arg_keys[5], 71), 0)
    return dict(patterns=patterns, background=background, offsets=offsets, probe_wave=probe_wave, object_field=object_field)


def dft_tables(side_len):
    indices = jnp.arange(side_len, dtype=jnp.int32)
    phases = indices[:, None] * indices[None, :] % side_len
    angles = phases.astype(jnp.float32) * jnp.float32(2.0 * math.pi / side_len)
    scaling = jnp.float32(1.0 / math.sqrt(side_len))
    return ((jnp.cos(angles) * scaling).astype(jnp.bfloat16), (-jnp.sin(angles) * scaling).astype(jnp.bfloat16))

def block_tables(real_part, imag_part):
    left_table = jnp.stack([jnp.stack([real_part, -imag_part]), jnp.stack([imag_part, real_part])])
    right_table = jnp.stack([jnp.stack([real_part, imag_part]), jnp.stack([-imag_part, real_part])])
    return (left_table, right_table)

def product(leading, trailing):
    real_part = leading[..., 0, :, :] * trailing[..., 0, :, :] - leading[..., 1, :, :] * trailing[..., 1, :, :]
    imag_part = leading[..., 0, :, :] * trailing[..., 1, :, :] + leading[..., 1, :, :] * trailing[..., 0, :, :]
    return jnp.stack([real_part, imag_part], axis=-3)

def times_conj(leading, trailing):
    real_part = leading[..., 0, :, :] * trailing[..., 0, :, :] + leading[..., 1, :, :] * trailing[..., 1, :, :]
    imag_part = leading[..., 0, :, :] * trailing[..., 1, :, :] - leading[..., 1, :, :] * trailing[..., 0, :, :]
    return jnp.stack([real_part, imag_part], axis=-3)

def transform(wave_set, left_table, right_table):
    half_way = jnp.einsum('cdkj,djn->ckn', left_table.astype(jnp.float32), wave_set.astype(jnp.float32), precision=lax.Precision.HIGHEST).astype(jnp.bfloat16)
    return jnp.einsum('ckn,cdnm->dkm', half_way.astype(jnp.float32), right_table.astype(jnp.float32), precision=lax.Precision.HIGHEST)

def reference(patterns, background, offsets, probe_wave, object_field):
    margin = K // 2
    real_part, imag_part = dft_tables(K)
    forward = block_tables(real_part, imag_part)
    inverse = block_tables(real_part, -imag_part)
    start_rows = (jnp.arange(SR, dtype=jnp.int32)[:, None] * STEP + offsets[:, :, 0].astype(jnp.int32)).reshape(SR * SC).astype(jnp.int32)
    start_cols = (jnp.arange(SC, dtype=jnp.int32)[None, :] * STEP + offsets[:, :, 1].astype(jnp.int32)).reshape(SR * SC).astype(jnp.int32)
    amplitude = jnp.sqrt(jnp.maximum(patterns - background, 0.0)).reshape(SR * SC, K, K)
    for sweep in range(ITERS):
        padded = jnp.pad(object_field, ((0, 0), (margin, margin), (margin, margin)))
        illumination = probe_wave[0] * probe_wave[0] + probe_wave[1] * probe_wave[1]

        def visit(carry, position_item):
            intersection, gradient = carry
            row_start, col_start, amp_one = position_item
            row_start = row_start.astype(jnp.int32)
            col_start = col_start.astype(jnp.int32)
            channel_zero = jnp.int32(0)
            window = lax.dynamic_slice(padded, (channel_zero, row_start, col_start), (2, K, K))
            exit_wave = product(probe_wave, window)
            far_field = transform(exit_wave.astype(jnp.bfloat16), forward[0], forward[1])
            magnitude = jnp.sqrt(far_field[0] * far_field[0] + far_field[1] * far_field[1])
            projected = (far_field * (amp_one / jnp.maximum(magnitude, 0.5))[None]).astype(jnp.bfloat16)
            back_wave = transform(projected, inverse[0], inverse[1])
            difference = back_wave - exit_wave
            obj_term = jnp.concatenate([times_conj(probe_wave, difference), illumination[None]], axis=0)
            current = lax.dynamic_slice(intersection, (channel_zero, row_start, col_start), (3, K, K))
            intersection = lax.dynamic_update_slice(intersection, current + obj_term, (channel_zero, row_start, col_start))
            return ((intersection, gradient + times_conj(window, difference)), None)
        initial = (jnp.zeros((3, NR + K, NC + K), jnp.float32), jnp.zeros((2, K, K), jnp.float32))
        (intersection, gradient), _ = lax.scan(visit, initial, (start_rows, start_cols, amplitude))
        inner = intersection[:, margin:margin + NR, margin:margin + NC]
        new_object = object_field + inner[0:2] / (inner[2] + 1.0)
        spread = jnp.sqrt(jnp.mean(gradient * gradient) + 1e-06)
        probe_wave = probe_wave + gradient / spread
        object_field = new_object
    return (object_field, probe_wave)
```

```python
import functools
import math

import jax
import jax.numpy as jnp
import numpy as np
from jax import lax
from jax.experimental import pallas as pl
from jax.experimental.pallas import tpu as pltpu
from jax.sharding import PartitionSpec as P

STEP = 64
ITERS = 2
LANES = 128
F32 = jnp.float32
BF16 = jnp.bfloat16


def dft_parts(side_len):
    indices = np.arange(side_len, dtype=np.int32)
    phases = indices[:, None] * indices[None, :] % side_len
    angles = phases.astype(np.float32) * np.float32(2.0 * math.pi / side_len)
    scaling = np.float32(1.0 / math.sqrt(side_len))
    real = (np.cos(angles) * scaling).astype(jnp.bfloat16)
    imag = (-np.sin(angles) * scaling).astype(jnp.bfloat16)
    return np.stack([real, imag]).astype(np.float32)


def plan(rows, cols, side):
    half = 2 * side
    pairs = cols // 2
    by_row = half // rows
    by_pair = max(8, by_row // pairs)
    owners = by_row // by_pair
    sems = {"halo": 0, "fold_col": 8, "fold_row": 14, "pair": 20}
    sems["row_sum"] = 21
    sems["col_sum"] = sems["row_sum"] + rows - 1
    sems["col_all"] = sems["col_sum"] + pairs - 1
    sems["row_all"] = sems["col_all"] + pairs - 1
    sems["pair_all"] = sems["row_all"] + rows - 1
    count = sems["pair_all"] + 1
    return half, pairs, by_row, by_pair, owners, sems, count


def kernel(rows, cols, pos_rows, pos_cols, side, *refs):
    inputs, (tile_out, probe_out) = refs[:6], refs[6:8]
    (amp, pad, lpad, win, exit_b, half_b, far, probe) = refs[8:16]
    (patterns, background, offsets, probe_in, tables, left, right, in_sem) = refs[16:24]
    (tile_end, probe_end, out_sem) = refs[24:27]
    per_iter = [refs[27 + 11 * i : 38 + 11 * i] for i in range(ITERS)]
    half, pairs, by_row, by_pair, owners, sems, _ = plan(rows, cols, side)
    margin = side // 2
    wide = 3 * margin
    positions = pos_rows * pos_cols
    row, col = lax.axis_index("row"), lax.axis_index("col")
    parity = lax.rem(col, 2)
    mate = col + 1 - 2 * parity
    group = lax.div(col, 2)
    has_up, has_down = row > 0, row < rows - 1
    has_left, has_right = col > 0, col < cols - 1
    up, down = lax.max(row - 1, 0), lax.min(row + 1, rows - 1)
    before, after = lax.max(col - 1, 0), lax.min(col + 1, cols - 1)
    started = []

    def at(r, c):
        return {"row": r, "col": c}

    def when(cond, act):
        if cond is None:
            act()
        else:
            pl.when(cond)(act)

    def row_pos(d):
        return lax.rem(row + d, rows)

    def pair_pos(d):
        return lax.rem(group + d, pairs)

    barrier = pltpu.get_barrier_semaphore()

    def greet(device):
        pl.semaphore_signal(barrier, inc=1, device_id=device, device_id_type=pl.DeviceIdType.MESH)

    for d in range(1, rows):
        greet(at(row_pos(d), col))
    for d in range(1, pairs):
        greet(at(row, 2 * pair_pos(d) + parity))
    when(has_left, lambda: greet(at(row, before)))
    when(has_right, lambda: greet(at(row, after)))

    def lane_index(n):
        return lax.broadcasted_iota(jnp.int32, (n, LANES), 1)

    def starts(p):
        a, b = lax.div(p, pos_cols), lax.rem(p, pos_cols)
        return a * STEP + offsets[a, b, 0], b * STEP + offsets[a, b, 1]

    def spread_lanes(first, second, c0):
        keep = lane_index(first.shape[0]) >= c0
        turn = lax.rem(c0, LANES)
        first, second = pltpu.roll(first, turn, 1), pltpu.roll(second, turn, 1)
        zero = jnp.zeros_like(first)
        return (
            jnp.where(keep, first, zero),
            jnp.where(keep, second, first),
            jnp.where(keep, zero, second),
        )

    centre = per_iter[0][0].at[:, 1, margin : 2 * margin, :]
    homes = (patterns, background, offsets, probe_in, centre, tables)
    fetches = [pltpu.make_async_copy(a, b, in_sem.at[i]) for i, (a, b) in enumerate(zip(inputs, homes))]
    for i in (4, 3, 2, 0, 1, 5):
        fetches[i].start()
    for wide_ref in (it[0] for it in per_iter):
        zeros = jnp.zeros((2, 3, margin, LANES), F32)

        @pl.when(row == 0)
        def _():
            wide_ref[:, :, 0:margin, :] = zeros

        @pl.when(row == rows - 1)
        def _():
            wide_ref[:, :, 2 * margin : wide, :] = zeros

        @pl.when(col == 0)
        def _():
            wide_ref[:, 0] = jnp.zeros((2, wide, LANES), F32)

        @pl.when(col == cols - 1)
        def _():
            wide_ref[:, 2] = jnp.zeros((2, wide, LANES), F32)

    beside = lax.min(col, 1) + lax.min(cols - 1 - col, 1)
    fetches[4].wait()
    pl.semaphore_wait(barrier, rows - 1 + pairs - 1 + beside)

    def link(step):
        s_sem, r_sem = per_iter[step][9:11]

        def copy(src, dst, k, device):
            return pltpu.make_async_remote_copy(
                src_ref=src,
                dst_ref=dst,
                send_sem=s_sem.at[k],
                recv_sem=r_sem.at[k],
                device_id=device,
                device_id_type=pl.DeviceIdType.MESH,
            )

        def send(src, dst, k, device, cond=None):
            moved = copy(src, dst, k, device)
            when(cond, moved.start)
            started.append((cond, moved))

        def arrive(dst, k, cond=None):
            when(cond, copy(dst, dst, k, at(row, mate)).wait_recv)

        return send, arrive

    def thirds(step):
        return lambda j, s: per_iter[step][0].at[:, j, s * margin : (s + 1) * margin, :]

    def strip_on(step, s, cond):
        send, third = link(step)[0], thirds(step)
        base = sems["halo"] + 2 + s
        go_right = has_right if cond is None else jnp.logical_and(has_right, cond)
        go_left = has_left if cond is None else jnp.logical_and(has_left, cond)
        send(third(1, s), third(0, s), base, at(row, after), go_right)
        send(third(1, s), third(2, s), base + 3, at(row, before), go_left)

    def halo_out(step):
        send, third = link(step)[0], thirds(step)
        send(third(1, 1), third(1, 0), sems["halo"], at(down, col), has_down)
        send(third(1, 1), third(1, 2), sems["halo"] + 1, at(up, col), has_up)
        strip_on(step, 1, None)

    def halo_on(step):
        arrive, third = link(step)[1], thirds(step)
        arrive(third(1, 0), sems["halo"], has_up)
        strip_on(step, 0, has_up)
        arrive(third(1, 2), sems["halo"] + 1, has_down)
        strip_on(step, 2, has_down)

    def halo_end(step):
        arrive, third = link(step)[1], thirds(step)
        for s, cond in ((1, None), (0, has_up), (2, has_down)):
            base = sems["halo"] + 2 + s
            from_left = has_left if cond is None else jnp.logical_and(has_left, cond)
            from_right = has_right if cond is None else jnp.logical_and(has_right, cond)
            arrive(third(0, s), base, from_left)
            arrive(third(2, s), base + 3, from_right)

    for step in range(ITERS):
        wide_ref, acc, got_col, got_row, grad, got_pair, got_rows, got_cols, total, s_sem, r_sem = (
            per_iter[step]
        )
        last = step == ITERS - 1

        send, arrive = link(step)
        third = thirds(step)
        if step == 0:
            halo_out(step)

        if step == 0:
            for i in (0, 1, 2, 3):
                fetches[i].wait()
            for ch in range(2):
                for j in range(2):
                    at_row = (2 * ch + j) * side
                    probe[at_row : at_row + side, :] = probe_in[ch, :, j * LANES : (j + 1) * LANES]

            @pl.loop(0, positions)
            def _(p):
                a, b = lax.div(p, pos_cols), lax.rem(p, pos_cols)
                amp[p] = jnp.sqrt(jnp.maximum(patterns[a, b] - background[...], 0.0))
                edge = jnp.zeros((3, margin, LANES), F32)
                for lo in (0, wide):
                    lpad[p, :, lo : lo + margin, :] = edge
                    for ch in range(2):
                        pad[p, ch, :, lo : lo + margin, :] = edge

        chunk = 32

        @pl.loop(0, positions * (side // chunk))
        def _(i):
            p = lax.div(i, side // chunk)
            r = lax.rem(i, side // chunk) * chunk
            _, c0 = starts(p)
            light = []
            for j in range(2):
                pr = probe[pl.ds(pl.multiple_of(j * side + r, chunk), chunk), :]
                pi = probe[pl.ds(pl.multiple_of((2 + j) * side + r, chunk), chunk), :]
                light.append(pr * pr + pi * pi)
            for j, part in enumerate(spread_lanes(light[0], light[1], c0)):
                lpad[p, j, pl.ds(pl.multiple_of(margin + r, chunk), chunk), :] = part

        def gather(source, to):
            row_starts = [starts(p)[0] for p in range(positions)]

            @pl.loop(0, wide // 64)
            def _(i):
                r = i * 64
                for j in range(3):
                    parts = [source(p, j, pl.ds(margin - row_starts[p] + r, 64)) for p in range(positions)]
                    acc[to, j, pl.ds(pl.multiple_of(r, 64), 64), :] = functools.reduce(
                        lambda x, y: x + y, parts
                    )

        def fold_cols(ch):
            k = sems["fold_col"] + 2 * ch
            send(acc.at[ch, 2], got_col.at[0, ch], k, at(row, after), has_right)
            send(acc.at[ch, 0], got_col.at[1, ch], k + 1, at(row, before), has_left)

        def fold_rows(ch):
            k = sems["fold_col"] + 2 * ch
            for side_at, cond in ((0, has_left), (1, has_right)):
                arrive(got_col.at[side_at, ch], k + side_at, cond)

                @pl.when(cond)
                def _():
                    acc[ch, 1] += got_col[side_at, ch]

            k = sems["fold_row"] + 2 * ch
            send(acc.at[ch, 1, 2 * margin : wide], got_row.at[0, ch], k, at(down, col), has_down)
            send(acc.at[ch, 1, 0:margin], got_row.at[1, ch], k + 1, at(up, col), has_up)

        def fold_end(ch):
            k = sems["fold_row"] + 2 * ch
            for side_at, cond in ((0, has_up), (1, has_down)):
                arrive(got_row.at[side_at, ch], k + side_at, cond)

                @pl.when(cond)
                def _():
                    acc[ch, 1, margin : 2 * margin] += got_row[side_at, ch]

        gather(lambda p, j, rs: lpad[p, j, rs, :], 2)
        fold_cols(2)

        if step == 0:
            halo_on(step)
            fetches[5].wait()
            real, imag = tables[0].astype(BF16), tables[1].astype(BF16)
            less = (-tables[1]).astype(BF16)
            for to, (one, two, three, four) in (
                (left, (real, less, imag, real)),
                (right, (real, imag, less, real)),
            ):
                to[0:side, 0:side] = one
                to[0:side, side : 2 * side] = two
                to[side : 2 * side, 0:side] = three
                to[side : 2 * side, side : 2 * side] = four
        grad[...] = jnp.zeros_like(grad)
        halo_end(step)
        fold_rows(2)

        def probe_part(ch, j, r):
            return probe[pl.ds(pl.multiple_of((2 * ch + j) * side + r, chunk), chunk), :]

        @pl.loop(0, positions)
        def _(p):
            r0, c0 = starts(p)

            @pl.loop(0, side // chunk)
            def _(i):
                r = i * chunk
                rs = pl.ds(pl.multiple_of(r, chunk), chunk)
                inside = lane_index(chunk) < LANES - c0
                turn = lax.rem(2 * LANES - c0, LANES)
                parts = []
                for ch in range(2):
                    b = [
                        pltpu.roll(wide_ref[ch, j, pl.ds(r0 + r, chunk), :], turn, 1)
                        for j in range(3)
                    ]
                    parts.append([jnp.where(inside, b[j], b[j + 1]) for j in range(2)])
                for j in range(2):
                    wr, wi = parts[0][j], parts[1][j]
                    pr, pi = probe_part(0, j, r), probe_part(1, j, r)
                    lanes = slice(j * LANES, (j + 1) * LANES)
                    win[0, rs, lanes] = wr
                    win[1, rs, lanes] = wi
                    exit_b[rs, lanes] = (pr * wr - pi * wi).astype(BF16)
                    ri = pl.ds(pl.multiple_of(side + r, chunk), chunk)
                    exit_b[ri, lanes] = (pr * wi + pi * wr).astype(BF16)

            def transform(one, two):
                halfway = jnp.dot(one[...], exit_b[...], preferred_element_type=F32).astype(BF16)
                half_b[:, 0:side] = halfway[0:side]
                half_b[:, side : 2 * side] = halfway[side : 2 * side]
                far[...] = jnp.dot(half_b[...], two[...], preferred_element_type=F32)

            transform(left, right)

            @pl.loop(0, side // chunk)
            def _(i):
                r = i * chunk
                rs = pl.ds(pl.multiple_of(r, chunk), chunk)
                fr, fi = far[rs, 0:side], far[rs, side : 2 * side]
                scale = amp[p, rs, :] * lax.rsqrt(jnp.maximum(fr * fr + fi * fi, 0.25))
                exit_b[rs, :] = (fr * scale).astype(BF16)
                ri = pl.ds(pl.multiple_of(side + r, chunk), chunk)
                exit_b[ri, :] = (fi * scale).astype(BF16)

            transform(right, left)

            @pl.loop(0, side // chunk)
            def _(i):
                r = i * chunk
                rs = pl.ds(pl.multiple_of(r, chunk), chunk)
                terms = [[], []]
                for j in range(2):
                    lanes = slice(j * LANES, (j + 1) * LANES)
                    wr, wi = win[0, rs, lanes], win[1, rs, lanes]
                    pr, pi = probe_part(0, j, r), probe_part(1, j, r)
                    dr = far[rs, j * LANES : (j + 1) * LANES] - (pr * wr - pi * wi)
                    di = far[rs, side + j * LANES : side + (j + 1) * LANES] - (pr * wi + pi * wr)
                    terms[0].append(pr * dr + pi * di)
                    terms[1].append(pr * di - pi * dr)
                    to_r = pl.ds(pl.multiple_of(j * side + r, chunk), chunk)
                    to_i = pl.ds(pl.multiple_of((2 + j) * side + r, chunk), chunk)
                    grad[to_r, :] += wr * dr + wi * di
                    grad[to_i, :] += wr * di - wi * dr
                for ch in range(2):
                    for j, part in enumerate(spread_lanes(terms[ch][0], terms[ch][1], c0)):
                        pad[p, ch, j, pl.ds(pl.multiple_of(margin + r, chunk), chunk), :] = part

        def span(start, size):
            return pl.ds(pl.multiple_of(start, 8), size)

        mine, theirs = parity * half, (1 - parity) * half
        base_row = mine + row * by_row
        base_own = base_row + group * by_pair
        owns = None if owners == pairs else group < owners

        send(grad.at[span(theirs, half)], got_pair, sems["pair"], at(row, mate))
        for ch in range(2):
            gather(lambda p, j, rs, ch=ch: pad[p, ch, j, rs, :], ch)
            fold_cols(ch)
        arrive(got_pair, sems["pair"])
        grad[span(mine, half), :] += got_pair[...]

        for d in range(1, rows):
            piece = grad.at[span(mine + row_pos(d) * by_row, by_row)]
            send(piece, got_rows.at[d - 1], sems["row_sum"] + d - 1, at(row_pos(d), col))
        fold_rows(0)
        for d in range(1, rows):
            arrive(got_rows.at[d - 1], sems["row_sum"] + d - 1)
        summed = grad[span(base_row, by_row), :]
        for d in range(1, rows):
            summed += got_rows[d - 1]
        grad[span(base_row, by_row), :] = summed

        for d in range(1, pairs):
            to = pair_pos(d)
            cond = None if owners == pairs else to < owners
            piece = grad.at[span(base_row + lax.min(to, owners - 1) * by_pair, by_pair)]
            send(piece, got_cols.at[d - 1], sems["col_sum"] + d - 1, at(row, 2 * to + parity), cond)
        fold_rows(1)
        for d in range(1, pairs):
            arrive(got_cols.at[d - 1], sems["col_sum"] + d - 1, owns)

        def finish():
            own = grad[span(base_own, by_pair), :]
            for d in range(1, pairs):
                own += got_cols[d - 1]
            total[span(base_own, by_pair), :] = own

        when(owns, finish)

        for d in range(1, pairs):
            piece = total.at[span(base_row + lax.min(group, owners - 1) * by_pair, by_pair)]
            device = at(row, 2 * pair_pos(d) + parity)
            send(piece, piece, sems["col_all"] + d - 1, device, owns)

        middle = slice(margin, 2 * margin)
        fold_end(2)
        for ch in range(2):
            fold_end(ch)
            changed = wide_ref[ch, 1, middle] + acc[ch, 1, middle] / (acc[2, 1, middle] + 1.0)
            if last:
                tile_end[ch] = changed
            else:
                per_iter[step + 1][0][ch, 1, middle] = changed
        if last:
            leaving = pltpu.make_async_copy(tile_end, tile_out, out_sem.at[0])
            leaving.start()
        else:
            halo_out(step + 1)

        for d in range(1, pairs):
            origin = pair_pos(pairs - d)
            cond = None if owners == pairs else origin < owners
            piece = total.at[span(base_row + lax.min(origin, owners - 1) * by_pair, by_pair)]
            arrive(piece, sems["col_all"] + d - 1, cond)
        for d in range(1, rows):
            piece = total.at[span(base_row, by_row)]
            send(piece, piece, sems["row_all"] + d - 1, at(row_pos(d), col))
        for d in range(1, rows):
            piece = total.at[span(mine + row_pos(rows - d) * by_row, by_row)]
            arrive(piece, sems["row_all"] + d - 1)
        piece = total.at[span(mine, half)]
        send(piece, piece, sems["pair_all"], at(row, mate))
        if not last:
            halo_on(step + 1)
        arrive(total.at[span(theirs, half)], sems["pair_all"])

        squares = jnp.zeros((8, LANES), F32)
        for i in range(4 * side // LANES):
            one = total[i * LANES : (i + 1) * LANES, :]
            squares += jnp.sum((one * one).reshape(LANES // 8, 8, LANES), axis=0)
        mean = jnp.sum(squares, keepdims=True) / (4 * side * LANES)
        scale = lax.rsqrt(mean + 1e-06)
        for ch in range(2):
            for j in range(2):
                at_row = (2 * ch + j) * side
                changed = probe[at_row : at_row + side, :] + total[at_row : at_row + side, :] * scale
                if last:
                    probe_end[ch, :, j * LANES : (j + 1) * LANES] = changed
                else:
                    probe[at_row : at_row + side, :] = changed

    parting = pltpu.make_async_copy(probe_end, probe_out, out_sem.at[1])
    parting.start()
    for cond, moved in started:
        when(cond, moved.wait_send)
    leaving.wait()
    parting.wait()


def on_device(rows, cols, patterns, background, offsets, probe_wave, object_field):
    side = probe_wave.shape[-1]
    margin = side // 2
    wide = 3 * margin
    pos_rows, pos_cols = patterns.shape[0], patterns.shape[1]
    positions = pos_rows * pos_cols
    assert object_field.shape[1:] == (margin, LANES) and margin == LANES
    assert side == 2 * LANES and pos_rows * STEP == margin and pos_cols * STEP == LANES
    half, pairs, by_row, by_pair, _, _, count = plan(rows, cols, side)
    tables = dft_parts(side)
    scratch = [
        pltpu.VMEM((positions, side, side), F32),
        pltpu.VMEM((positions, 2, 3, wide + margin, LANES), F32),
        pltpu.VMEM((positions, 3, wide + margin, LANES), F32),
        pltpu.VMEM((2, side, side), F32),
        pltpu.VMEM((2 * side, side), BF16),
        pltpu.VMEM((side, 2 * side), BF16),
        pltpu.VMEM((side, 2 * side), F32),
        pltpu.VMEM((4 * side, LANES), F32),
        pltpu.VMEM(patterns.shape, F32),
        pltpu.VMEM(background.shape, F32),
        pltpu.SMEM(offsets.shape, jnp.int32),
        pltpu.VMEM(probe_wave.shape, F32),
        pltpu.VMEM(tables.shape, F32),
        pltpu.VMEM((2 * side, 2 * side), BF16),
        pltpu.VMEM((2 * side, 2 * side), BF16),
        pltpu.SemaphoreType.DMA((6,)),
        pltpu.VMEM(object_field.shape, F32),
        pltpu.VMEM(probe_wave.shape, F32),
        pltpu.SemaphoreType.DMA((2,)),
    ]
    for _ in range(ITERS):
        scratch += [
            pltpu.VMEM((2, 3, wide, LANES), F32),
            pltpu.VMEM((3, 3, wide, LANES), F32),
            pltpu.VMEM((2, 3, wide, LANES), F32),
            pltpu.VMEM((2, 3, margin, LANES), F32),
            pltpu.VMEM((4 * side, LANES), F32),
            pltpu.VMEM((half, LANES), F32),
            pltpu.VMEM((rows - 1, by_row, LANES), F32),
            pltpu.VMEM((pairs - 1, by_pair, LANES), F32),
            pltpu.VMEM((4 * side, LANES), F32),
            pltpu.SemaphoreType.DMA((count,)),
            pltpu.SemaphoreType.DMA((count,)),
        ]
    in_hbm = pl.BlockSpec(memory_space=pltpu.HBM)
    return pl.pallas_call(
        functools.partial(kernel, rows, cols, pos_rows, pos_cols, side),
        out_shape=(
            jax.ShapeDtypeStruct(object_field.shape, F32),
            jax.ShapeDtypeStruct(probe_wave.shape, F32),
        ),
        in_specs=[in_hbm] * 6,
        out_specs=(in_hbm, in_hbm),
        scratch_shapes=scratch,
        compiler_params=pltpu.CompilerParams(
            collective_id=0, has_side_effects=True, vmem_limit_bytes=60 * 1024 * 1024
        ),
    )(patterns, background, offsets, probe_wave, object_field, jnp.asarray(tables))


def solution(mesh):
    placed = (P("row", "col", None, None), P(), P("row", "col", None), P(), P(None, "row", "col"))
    return jax.shard_map(
        functools.partial(on_device, mesh.shape["row"], mesh.shape["col"]),
        mesh=mesh,
        in_specs=placed,
        out_specs=(P(None, "row", "col"), P()),
        check_vma=False,
    )
```

```python
import functools
import math

import jax
import jax.numpy as jnp
import numpy as np
from jax import lax
from jax.experimental import pallas as pl
from jax.experimental.pallas import tpu as pltpu
from jax.sharding import PartitionSpec as P

STEP = 64
ITERS = 2
LANES = 128
F32 = jnp.float32
BF16 = jnp.bfloat16


def dft_parts(side_len):
    indices = np.arange(side_len, dtype=np.int32)
    phases = indices[:, None] * indices[None, :] % side_len
    angles = phases.astype(np.float32) * np.float32(2.0 * math.pi / side_len)
    scaling = np.float32(1.0 / math.sqrt(side_len))
    real = (np.cos(angles) * scaling).astype(jnp.bfloat16)
    imag = (-np.sin(angles) * scaling).astype(jnp.bfloat16)
    return np.stack([real, imag]).astype(np.float32)


def plan(rows, cols, side):
    half = 2 * side
    pairs = cols // 2
    by_row = half // rows
    by_pair = max(8, by_row // pairs)
    owners = by_row // by_pair
    sems = {"halo": 0, "fold_col": 8, "fold_row": 14, "pair": 20}
    sems["row_sum"] = 21
    sems["col_sum"] = sems["row_sum"] + rows - 1
    sems["col_all"] = sems["col_sum"] + pairs - 1
    sems["row_all"] = sems["col_all"] + pairs - 1
    sems["pair_all"] = sems["row_all"] + rows - 1
    count = sems["pair_all"] + 1
    return half, pairs, by_row, by_pair, owners, sems, count


def kernel(rows, cols, pos_rows, pos_cols, side, *refs):
    inputs, (tile_out, probe_out) = refs[:6], refs[6:8]
    (amp, pad, lpad, win, exit_b, half_b, far, probe) = refs[8:16]
    (patterns, background, offsets, probe_in, tables, left, right, in_sem) = refs[16:24]
    (tile_end, probe_end, out_sem) = refs[24:27]
    per_iter = [refs[27 + 11 * i : 38 + 11 * i] for i in range(ITERS)]
    half, pairs, by_row, by_pair, owners, sems, _ = plan(rows, cols, side)
    margin = side // 2
    wide = 3 * margin
    positions = pos_rows * pos_cols
    row, col = lax.axis_index("row"), lax.axis_index("col")
    parity = lax.rem(col, 2)
    mate = col + 1 - 2 * parity
    group = lax.div(col, 2)
    has_up, has_down = row > 0, row < rows - 1
    has_left, has_right = col > 0, col < cols - 1
    up, down = lax.max(row - 1, 0), lax.min(row + 1, rows - 1)
    before, after = lax.max(col - 1, 0), lax.min(col + 1, cols - 1)
    started = []

    def at(r, c):
        return {"row": r, "col": c}

    def when(cond, act):
        if cond is None:
            act()
        else:
            pl.when(cond)(act)

    def row_pos(d):
        return lax.rem(row + d, rows)

    def pair_pos(d):
        return lax.rem(group + d, pairs)

    barrier = pltpu.get_barrier_semaphore()

    def greet(device):
        pl.semaphore_signal(barrier, inc=1, device_id=device, device_id_type=pl.DeviceIdType.MESH)

    for d in range(1, rows):
        greet(at(row_pos(d), col))
    for d in range(1, pairs):
        greet(at(row, 2 * pair_pos(d) + parity))
    when(has_left, lambda: greet(at(row, before)))
    when(has_right, lambda: greet(at(row, after)))

    def lane_index(n):
        return lax.broadcasted_iota(jnp.int32, (n, LANES), 1)

    def starts(p):
        a, b = lax.div(p, pos_cols), lax.rem(p, pos_cols)
        return a * STEP + offsets[a, b, 0], b * STEP + offsets[a, b, 1]

    def spread_lanes(first, second, c0):
        keep = lane_index(first.shape[0]) >= c0
        turn = lax.rem(c0, LANES)
        first, second = pltpu.roll(first, turn, 1), pltpu.roll(second, turn, 1)
        zero = jnp.zeros_like(first)
        return (
            jnp.where(keep, first, zero),
            jnp.where(keep, second, first),
            jnp.where(keep, zero, second),
        )

    centre = per_iter[0][0].at[:, 1, margin : 2 * margin, :]
    homes = (patterns, background, offsets, probe_in, centre, tables)
    fetches = [pltpu.make_async_copy(a, b, in_sem.at[i]) for i, (a, b) in enumerate(zip(inputs, homes))]
    for i in (4, 3, 2, 0, 1, 5):
        fetches[i].start()
    for wide_ref in (it[0] for it in per_iter):
        zeros = jnp.zeros((2, 3, margin, LANES), F32)

        @pl.when(row == 0)
        def _():
            wide_ref[:, :, 0:margin, :] = zeros

        @pl.when(row == rows - 1)
        def _():
            wide_ref[:, :, 2 * margin : wide, :] = zeros

        @pl.when(col == 0)
        def _():
            wide_ref[:, 0] = jnp.zeros((2, wide, LANES), F32)

        @pl.when(col == cols - 1)
        def _():
            wide_ref[:, 2] = jnp.zeros((2, wide, LANES), F32)

    beside = lax.min(col, 1) + lax.min(cols - 1 - col, 1)
    fetches[4].wait()
    pl.semaphore_wait(barrier, rows - 1 + pairs - 1 + beside)

    def link(step):
        s_sem, r_sem = per_iter[step][9:11]

        def copy(src, dst, k, device):
            return pltpu.make_async_remote_copy(
                src_ref=src,
                dst_ref=dst,
                send_sem=s_sem.at[k],
                recv_sem=r_sem.at[k],
                device_id=device,
                device_id_type=pl.DeviceIdType.MESH,
            )

        def send(src, dst, k, device, cond=None):
            moved = copy(src, dst, k, device)
            when(cond, moved.start)
            started.append((cond, moved))

        def arrive(dst, k, cond=None):
            when(cond, copy(dst, dst, k, at(row, mate)).wait_recv)

        return send, arrive

    def thirds(step):
        return lambda j, s: per_iter[step][0].at[:, j, s * margin : (s + 1) * margin, :]

    def strip_on(step, s, cond):
        send, third = link(step)[0], thirds(step)
        base = sems["halo"] + 2 + s
        go_right = has_right if cond is None else jnp.logical_and(has_right, cond)
        go_left = has_left if cond is None else jnp.logical_and(has_left, cond)
        send(third(1, s), third(0, s), base, at(row, after), go_right)
        send(third(1, s), third(2, s), base + 3, at(row, before), go_left)

    def halo_out(step):
        send, third = link(step)[0], thirds(step)
        send(third(1, 1), third(1, 0), sems["halo"], at(down, col), has_down)
        send(third(1, 1), third(1, 2), sems["halo"] + 1, at(up, col), has_up)
        strip_on(step, 1, None)

    def halo_on(step):
        arrive, third = link(step)[1], thirds(step)
        arrive(third(1, 0), sems["halo"], has_up)
        strip_on(step, 0, has_up)
        arrive(third(1, 2), sems["halo"] + 1, has_down)
        strip_on(step, 2, has_down)

    def halo_end(step):
        arrive, third = link(step)[1], thirds(step)
        for s, cond in ((1, None), (0, has_up), (2, has_down)):
            base = sems["halo"] + 2 + s
            from_left = has_left if cond is None else jnp.logical_and(has_left, cond)
            from_right = has_right if cond is None else jnp.logical_and(has_right, cond)
            arrive(third(0, s), base, from_left)
            arrive(third(2, s), base + 3, from_right)

    for step in range(ITERS):
        wide_ref, acc, got_col, got_row, grad, got_pair, got_rows, got_cols, total, s_sem, r_sem = (
            per_iter[step]
        )
        last = step == ITERS - 1

        send, arrive = link(step)
        third = thirds(step)
        if step == 0:
            halo_out(step)

        if step == 0:
            for i in (2, 3):
                fetches[i].wait()
            for ch in range(2):
                for j in range(2):
                    at_row = (2 * ch + j) * side
                    probe[at_row : at_row + side, :] = probe_in[ch, :, j * LANES : (j + 1) * LANES]

            halo_on(step)
            for i in (0, 1):
                fetches[i].wait()

            @pl.loop(0, positions)
            def _(p):
                a, b = lax.div(p, pos_cols), lax.rem(p, pos_cols)
                amp[p] = jnp.sqrt(jnp.maximum(patterns[a, b] - background[...], 0.0))
                edge = jnp.zeros((3, margin, LANES), F32)
                for lo in (0, wide):
                    lpad[p, :, lo : lo + margin, :] = edge
                    for ch in range(2):
                        pad[p, ch, :, lo : lo + margin, :] = edge

        chunk = 32

        @pl.loop(0, side // chunk)
        def _(i):
            r = i * chunk
            light = []
            for j in range(2):
                pr = probe[pl.ds(pl.multiple_of(j * side + r, chunk), chunk), :]
                pi = probe[pl.ds(pl.multiple_of((2 + j) * side + r, chunk), chunk), :]
                light.append(pr * pr + pi * pi)
            for p in range(positions):
                for j, part in enumerate(spread_lanes(light[0], light[1], starts(p)[1])):
                    lpad[p, j, pl.ds(pl.multiple_of(margin + r, chunk), chunk), :] = part

        def gather(source, to):
            row_starts = [starts(p)[0] for p in range(positions)]

            @pl.loop(0, wide // 64)
            def _(i):
                r = i * 64
                for j in range(3):
                    parts = [source(p, j, pl.ds(margin - row_starts[p] + r, 64)) for p in range(positions)]
                    acc[to, j, pl.ds(pl.multiple_of(r, 64), 64), :] = functools.reduce(
                        lambda x, y: x + y, parts
                    )

        def fold_cols(ch):
            k = sems["fold_col"] + 2 * ch
            send(acc.at[ch, 2], got_col.at[0, ch], k, at(row, after), has_right)
            send(acc.at[ch, 0], got_col.at[1, ch], k + 1, at(row, before), has_left)

        def fold_rows(ch):
            k = sems["fold_col"] + 2 * ch
            for side_at, cond in ((0, has_left), (1, has_right)):
                arrive(got_col.at[side_at, ch], k + side_at, cond)

                @pl.when(cond)
                def _():
                    acc[ch, 1] += got_col[side_at, ch]

            k = sems["fold_row"] + 2 * ch
            send(acc.at[ch, 1, 2 * margin : wide], got_row.at[0, ch], k, at(down, col), has_down)
            send(acc.at[ch, 1, 0:margin], got_row.at[1, ch], k + 1, at(up, col), has_up)

        def fold_end(ch):
            k = sems["fold_row"] + 2 * ch
            for side_at, cond in ((0, has_up), (1, has_down)):
                arrive(got_row.at[side_at, ch], k + side_at, cond)

                @pl.when(cond)
                def _():
                    acc[ch, 1, margin : 2 * margin] += got_row[side_at, ch]

        gather(lambda p, j, rs: lpad[p, j, rs, :], 2)
        fold_cols(2)

        if step == 0:
            fetches[5].wait()
            real, imag = tables[0].astype(BF16), tables[1].astype(BF16)
            less = (-tables[1]).astype(BF16)
            for to, (one, two, three, four) in (
                (left, (real, less, imag, real)),
                (right, (real, imag, less, real)),
            ):
                to[0:side, 0:side] = one
                to[0:side, side : 2 * side] = two
                to[side : 2 * side, 0:side] = three
                to[side : 2 * side, side : 2 * side] = four
        grad[...] = jnp.zeros_like(grad)
        halo_end(step)
        fold_rows(2)

        def probe_part(ch, j, r):
            at_row = (2 * ch + j) * side + r
            return probe[at_row : at_row + chunk, :]

        def leave(p, q):
            r0, c0 = starts(p)
            inside = lane_index(chunk) < LANES - c0
            turn = lax.rem(2 * LANES - c0, LANES)
            for r in range(0, side, chunk):
                parts = []
                for ch in range(2):
                    b = [
                        pltpu.roll(wide_ref[ch, j, pl.ds(r0 + r, chunk), :], turn, 1)
                        for j in range(3)
                    ]
                    parts.append([jnp.where(inside, b[j], b[j + 1]) for j in range(2)])
                for j in range(2):
                    wr, wi = parts[0][j], parts[1][j]
                    pr, pi = probe_part(0, j, r), probe_part(1, j, r)
                    lanes = slice(j * LANES, (j + 1) * LANES)
                    win[q, 0, r : r + chunk, lanes] = wr
                    win[q, 1, r : r + chunk, lanes] = wi
                    exit_b[q, r : r + chunk, lanes] = (pr * wr - pi * wi).astype(BF16)
                    exit_b[q, side + r : side + r + chunk, lanes] = (pr * wi + pi * wr).astype(BF16)

        def transform(one, two, q):
            halfway = jnp.dot(one[...], exit_b[q], preferred_element_type=F32).astype(BF16)
            half_b[q, :, 0:side] = halfway[0:side]
            half_b[q, :, side : 2 * side] = halfway[side : 2 * side]
            far[q] = jnp.dot(half_b[q], two[...], preferred_element_type=F32)

        def project(p, q):
            for r in range(0, side, chunk):
                fr, fi = far[q, r : r + chunk, 0:side], far[q, r : r + chunk, side : 2 * side]
                scale = amp[p, r : r + chunk, :] * lax.rsqrt(jnp.maximum(fr * fr + fi * fi, 0.25))
                exit_b[q, r : r + chunk, :] = (fr * scale).astype(BF16)
                exit_b[q, side + r : side + r + chunk, :] = (fi * scale).astype(BF16)

        def collect(places):
            for r in range(0, side, chunk):
                rs = slice(r, r + chunk)
                terms = [[[], []] for _ in places]
                for j in range(2):
                    lanes = slice(j * LANES, (j + 1) * LANES)
                    pr, pi = probe_part(0, j, r), probe_part(1, j, r)
                    sums = [0.0, 0.0]
                    for p, q in places:
                        wr, wi = win[q, 0, rs, lanes], win[q, 1, rs, lanes]
                        dr = far[q, rs, lanes] - (pr * wr - pi * wi)
                        di = far[q, rs, side + j * LANES : side + (j + 1) * LANES]
                        di = di - (pr * wi + pi * wr)
                        terms[q][0].append(pr * dr + pi * di)
                        terms[q][1].append(pr * di - pi * dr)
                        sums[0] += wr * dr + wi * di
                        sums[1] += wr * di - wi * dr
                    for ch in range(2):
                        at_row = (2 * ch + j) * side + r
                        grad[at_row : at_row + chunk, :] += sums[ch]
                for p, q in places:
                    c0 = starts(p)[1]
                    for ch in range(2):
                        for j, part in enumerate(spread_lanes(terms[q][ch][0], terms[q][ch][1], c0)):
                            pad[p, ch, j, margin + r : margin + r + chunk, :] = part

        @pl.loop(0, positions // 2)
        def _(i):
            places = [(2 * i + q, q) for q in range(2)]
            for p, q in places:
                leave(p, q)
            for p, q in places:
                transform(left, right, q)
                project(p, q)
            for p, q in places:
                transform(right, left, q)
            collect(places)

        def span(start, size):
            return pl.ds(pl.multiple_of(start, 8), size)

        mine, theirs = parity * half, (1 - parity) * half
        base_row = mine + row * by_row
        base_own = base_row + group * by_pair
        owns = None if owners == pairs else group < owners

        send(grad.at[span(theirs, half)], got_pair, sems["pair"], at(row, mate))
        for ch in range(2):
            gather(lambda p, j, rs, ch=ch: pad[p, ch, j, rs, :], ch)
            fold_cols(ch)
        arrive(got_pair, sems["pair"])
        grad[span(mine, half), :] += got_pair[...]

        for d in range(1, rows):
            piece = grad.at[span(mine + row_pos(d) * by_row, by_row)]
            send(piece, got_rows.at[d - 1], sems["row_sum"] + d - 1, at(row_pos(d), col))
        fold_rows(0)
        for d in range(1, rows):
            arrive(got_rows.at[d - 1], sems["row_sum"] + d - 1)
        summed = grad[span(base_row, by_row), :]
        for d in range(1, rows):
            summed += got_rows[d - 1]
        grad[span(base_row, by_row), :] = summed

        for d in range(1, pairs):
            to = pair_pos(d)
            cond = None if owners == pairs else to < owners
            piece = grad.at[span(base_row + lax.min(to, owners - 1) * by_pair, by_pair)]
            send(piece, got_cols.at[d - 1], sems["col_sum"] + d - 1, at(row, 2 * to + parity), cond)
        fold_rows(1)
        for d in range(1, pairs):
            arrive(got_cols.at[d - 1], sems["col_sum"] + d - 1, owns)

        def finish():
            own = grad[span(base_own, by_pair), :]
            for d in range(1, pairs):
                own += got_cols[d - 1]
            total[span(base_own, by_pair), :] = own

        when(owns, finish)

        for d in range(1, pairs):
            piece = total.at[span(base_row + lax.min(group, owners - 1) * by_pair, by_pair)]
            device = at(row, 2 * pair_pos(d) + parity)
            send(piece, piece, sems["col_all"] + d - 1, device, owns)

        middle = slice(margin, 2 * margin)
        fold_end(2)
        for ch in range(2):
            fold_end(ch)
            changed = wide_ref[ch, 1, middle] + acc[ch, 1, middle] / (acc[2, 1, middle] + 1.0)
            if last:
                tile_end[ch] = changed
            else:
                per_iter[step + 1][0][ch, 1, middle] = changed
        if last:
            leaving = pltpu.make_async_copy(tile_end, tile_out, out_sem.at[0])
            leaving.start()
        else:
            halo_out(step + 1)

        for d in range(1, pairs):
            origin = pair_pos(pairs - d)
            cond = None if owners == pairs else origin < owners
            piece = total.at[span(base_row + lax.min(origin, owners - 1) * by_pair, by_pair)]
            arrive(piece, sems["col_all"] + d - 1, cond)
        for d in range(1, rows):
            piece = total.at[span(base_row, by_row)]
            send(piece, piece, sems["row_all"] + d - 1, at(row_pos(d), col))
        for d in range(1, rows):
            piece = total.at[span(mine + row_pos(rows - d) * by_row, by_row)]
            arrive(piece, sems["row_all"] + d - 1)
        piece = total.at[span(mine, half)]
        send(piece, piece, sems["pair_all"], at(row, mate))
        if not last:
            halo_on(step + 1)
        arrive(total.at[span(theirs, half)], sems["pair_all"])

        squares = jnp.zeros((8, LANES), F32)
        for i in range(4 * side // LANES):
            one = total[i * LANES : (i + 1) * LANES, :]
            squares += jnp.sum((one * one).reshape(LANES // 8, 8, LANES), axis=0)
        mean = jnp.sum(squares, keepdims=True) / (4 * side * LANES)
        scale = lax.rsqrt(mean + 1e-06)
        for ch in range(2):
            for j in range(2):
                at_row = (2 * ch + j) * side
                changed = probe[at_row : at_row + side, :] + total[at_row : at_row + side, :] * scale
                if last:
                    probe_end[ch, :, j * LANES : (j + 1) * LANES] = changed
                else:
                    probe[at_row : at_row + side, :] = changed

    parting = pltpu.make_async_copy(probe_end, probe_out, out_sem.at[1])
    parting.start()
    for cond, moved in started:
        when(cond, moved.wait_send)
    leaving.wait()
    parting.wait()


def on_device(rows, cols, patterns, background, offsets, probe_wave, object_field):
    side = probe_wave.shape[-1]
    margin = side // 2
    wide = 3 * margin
    pos_rows, pos_cols = patterns.shape[0], patterns.shape[1]
    positions = pos_rows * pos_cols
    assert object_field.shape[1:] == (margin, LANES) and margin == LANES
    assert positions % 2 == 0 and side == 2 * LANES and pos_rows * STEP == margin and pos_cols * STEP == LANES
    half, pairs, by_row, by_pair, _, _, count = plan(rows, cols, side)
    tables = dft_parts(side)
    scratch = [
        pltpu.VMEM((positions, side, side), F32),
        pltpu.VMEM((positions, 2, 3, wide + margin, LANES), F32),
        pltpu.VMEM((positions, 3, wide + margin, LANES), F32),
        pltpu.VMEM((2, 2, side, side), F32),
        pltpu.VMEM((2, 2 * side, side), BF16),
        pltpu.VMEM((2, side, 2 * side), BF16),
        pltpu.VMEM((2, side, 2 * side), F32),
        pltpu.VMEM((4 * side, LANES), F32),
        pltpu.VMEM(patterns.shape, F32),
        pltpu.VMEM(background.shape, F32),
        pltpu.SMEM(offsets.shape, jnp.int32),
        pltpu.VMEM(probe_wave.shape, F32),
        pltpu.VMEM(tables.shape, F32),
        pltpu.VMEM((2 * side, 2 * side), BF16),
        pltpu.VMEM((2 * side, 2 * side), BF16),
        pltpu.SemaphoreType.DMA((6,)),
        pltpu.VMEM(object_field.shape, F32),
        pltpu.VMEM(probe_wave.shape, F32),
        pltpu.SemaphoreType.DMA((2,)),
    ]
    for _ in range(ITERS):
        scratch += [
            pltpu.VMEM((2, 3, wide, LANES), F32),
            pltpu.VMEM((3, 3, wide, LANES), F32),
            pltpu.VMEM((2, 3, wide, LANES), F32),
            pltpu.VMEM((2, 3, margin, LANES), F32),
            pltpu.VMEM((4 * side, LANES), F32),
            pltpu.VMEM((half, LANES), F32),
            pltpu.VMEM((rows - 1, by_row, LANES), F32),
            pltpu.VMEM((pairs - 1, by_pair, LANES), F32),
            pltpu.VMEM((4 * side, LANES), F32),
            pltpu.SemaphoreType.DMA((count,)),
            pltpu.SemaphoreType.DMA((count,)),
        ]
    in_hbm = pl.BlockSpec(memory_space=pltpu.HBM)
    return pl.pallas_call(
        functools.partial(kernel, rows, cols, pos_rows, pos_cols, side),
        out_shape=(
            jax.ShapeDtypeStruct(object_field.shape, F32),
            jax.ShapeDtypeStruct(probe_wave.shape, F32),
        ),
        in_specs=[in_hbm] * 6,
        out_specs=(in_hbm, in_hbm),
        scratch_shapes=scratch,
        compiler_params=pltpu.CompilerParams(
            collective_id=0, has_side_effects=True, vmem_limit_bytes=60 * 1024 * 1024
        ),
    )(patterns, background, offsets, probe_wave, object_field, jnp.asarray(tables))


def solution(mesh):
    placed = (P("row", "col", None, None), P(), P("row", "col", None), P(), P(None, "row", "col"))
    return jax.shard_map(
        functools.partial(on_device, mesh.shape["row"], mesh.shape["col"]),
        mesh=mesh,
        in_specs=placed,
        out_specs=(P(None, "row", "col"), P()),
        check_vma=False,
    )
```

```python
import functools
import math

import jax
import jax.numpy as jnp
import numpy as np
from jax import lax
from jax.experimental import pallas as pl
from jax.experimental.pallas import tpu as pltpu
from jax.sharding import PartitionSpec as P

STEP = 64
ITERS = 2
LANES = 128
F32 = jnp.float32
BF16 = jnp.bfloat16


def dft_parts(side_len):
    indices = np.arange(side_len, dtype=np.int32)
    phases = indices[:, None] * indices[None, :] % side_len
    angles = phases.astype(np.float32) * np.float32(2.0 * math.pi / side_len)
    scaling = np.float32(1.0 / math.sqrt(side_len))
    real = (np.cos(angles) * scaling).astype(jnp.bfloat16)
    imag = (-np.sin(angles) * scaling).astype(jnp.bfloat16)
    return np.stack([real, imag]).astype(np.float32)


def plan(rows, cols, side):
    half = 2 * side
    pairs = cols // 2
    by_row = half // rows
    by_pair = max(8, by_row // pairs)
    owners = by_row // by_pair
    sems = {"halo": 0, "fold_col": 8, "fold_row": 26, "pair": 32}
    sems["row_sum"] = 33
    sems["col_sum"] = sems["row_sum"] + rows - 1
    sems["col_all"] = sems["col_sum"] + pairs - 1
    sems["row_all"] = sems["col_all"] + pairs - 1
    sems["pair_all"] = sems["row_all"] + rows - 1
    count = sems["pair_all"] + rows
    return half, pairs, by_row, by_pair, owners, sems, count


def kernel(rows, cols, pos_rows, pos_cols, side, *refs):
    inputs, (tile_out, probe_out) = refs[:6], refs[6:8]
    (amp, pad, lpad, win, exit_b, half_b, far, probe) = refs[8:16]
    (patterns, background, offsets, probe_in, tables, left, right, in_sem) = refs[16:24]
    (tile_end, probe_end, out_sem) = refs[24:27]
    per_iter = [refs[27 + 11 * i : 38 + 11 * i] for i in range(ITERS)]
    half, pairs, by_row, by_pair, owners, sems, _ = plan(rows, cols, side)
    margin = side // 2
    wide = 3 * margin
    positions = pos_rows * pos_cols
    row, col = lax.axis_index("row"), lax.axis_index("col")
    parity = lax.rem(col, 2)
    mate = col + 1 - 2 * parity
    group = lax.div(col, 2)
    has_up, has_down = row > 0, row < rows - 1
    has_left, has_right = col > 0, col < cols - 1
    up, down = lax.max(row - 1, 0), lax.min(row + 1, rows - 1)
    before, after = lax.max(col - 1, 0), lax.min(col + 1, cols - 1)
    started = []

    def at(r, c):
        return {"row": r, "col": c}

    def when(cond, act):
        if cond is None:
            act()
        else:
            pl.when(cond)(act)

    def row_pos(d):
        return lax.rem(row + d, rows)

    def pair_pos(d):
        return lax.rem(group + d, pairs)

    barrier = pltpu.get_barrier_semaphore()

    def greet(device):
        pl.semaphore_signal(barrier, inc=1, device_id=device, device_id_type=pl.DeviceIdType.MESH)

    for d in range(1, rows):
        greet(at(row_pos(d), col))
    for d in range(1, pairs):
        greet(at(row, 2 * pair_pos(d) + parity))
    when(has_left, lambda: greet(at(row, before)))
    when(has_right, lambda: greet(at(row, after)))

    def lane_index(n):
        return lax.broadcasted_iota(jnp.int32, (n, LANES), 1)

    def starts(p):
        a, b = lax.div(p, pos_cols), lax.rem(p, pos_cols)
        return a * STEP + offsets[a, b, 0], b * STEP + offsets[a, b, 1]

    def spread_lanes(first, second, c0):
        keep = lane_index(first.shape[0]) >= c0
        turn = lax.rem(c0, LANES)
        first, second = pltpu.roll(first, turn, 1), pltpu.roll(second, turn, 1)
        zero = jnp.zeros_like(first)
        return (
            jnp.where(keep, first, zero),
            jnp.where(keep, second, first),
            jnp.where(keep, zero, second),
        )

    centre = per_iter[0][0].at[:, 1, margin : 2 * margin, :]
    homes = (patterns, background, offsets, probe_in, centre, tables)
    fetches = [pltpu.make_async_copy(a, b, in_sem.at[i]) for i, (a, b) in enumerate(zip(inputs, homes))]
    for i in (4, 3, 2, 0, 1, 5):
        fetches[i].start()
    for wide_ref in (it[0] for it in per_iter):
        zeros = jnp.zeros((2, 3, margin, LANES), F32)

        @pl.when(row == 0)
        def _():
            wide_ref[:, :, 0:margin, :] = zeros

        @pl.when(row == rows - 1)
        def _():
            wide_ref[:, :, 2 * margin : wide, :] = zeros

        @pl.when(col == 0)
        def _():
            wide_ref[:, 0] = jnp.zeros((2, wide, LANES), F32)

        @pl.when(col == cols - 1)
        def _():
            wide_ref[:, 2] = jnp.zeros((2, wide, LANES), F32)

    beside = lax.min(col, 1) + lax.min(cols - 1 - col, 1)
    fetches[4].wait()
    pl.semaphore_wait(barrier, rows - 1 + pairs - 1 + beside)

    def link(step):
        s_sem, r_sem = per_iter[step][9:11]

        def copy(src, dst, k, device):
            return pltpu.make_async_remote_copy(
                src_ref=src,
                dst_ref=dst,
                send_sem=s_sem.at[k],
                recv_sem=r_sem.at[k],
                device_id=device,
                device_id_type=pl.DeviceIdType.MESH,
            )

        def send(src, dst, k, device, cond=None):
            moved = copy(src, dst, k, device)
            when(cond, moved.start)
            started.append((cond, moved))

        def arrive(dst, k, cond=None):
            when(cond, copy(dst, dst, k, at(row, mate)).wait_recv)

        return send, arrive

    def thirds(step):
        return lambda j, s: per_iter[step][0].at[:, j, s * margin : (s + 1) * margin, :]

    def strip_on(step, s, cond):
        send, third = link(step)[0], thirds(step)
        base = sems["halo"] + 2 + s
        go_right = has_right if cond is None else jnp.logical_and(has_right, cond)
        go_left = has_left if cond is None else jnp.logical_and(has_left, cond)
        send(third(1, s), third(0, s), base, at(row, after), go_right)
        send(third(1, s), third(2, s), base + 3, at(row, before), go_left)

    def halo_out(step):
        send, third = link(step)[0], thirds(step)
        send(third(1, 1), third(1, 0), sems["halo"], at(down, col), has_down)
        send(third(1, 1), third(1, 2), sems["halo"] + 1, at(up, col), has_up)
        strip_on(step, 1, None)

    def halo_on(step):
        arrive, third = link(step)[1], thirds(step)
        arrive(third(1, 0), sems["halo"], has_up)
        strip_on(step, 0, has_up)
        arrive(third(1, 2), sems["halo"] + 1, has_down)
        strip_on(step, 2, has_down)

    def halo_end(step):
        arrive, third = link(step)[1], thirds(step)
        for s, cond in ((1, None), (0, has_up), (2, has_down)):
            base = sems["halo"] + 2 + s
            from_left = has_left if cond is None else jnp.logical_and(has_left, cond)
            from_right = has_right if cond is None else jnp.logical_and(has_right, cond)
            arrive(third(0, s), base, from_left)
            arrive(third(2, s), base + 3, from_right)

    for step in range(ITERS):
        wide_ref, acc, got_col, got_row, grad, got_pair, got_rows, got_cols, total, s_sem, r_sem = (
            per_iter[step]
        )
        last = step == ITERS - 1

        send, arrive = link(step)
        third = thirds(step)
        if step == 0:
            halo_out(step)

        if step == 0:
            for i in (2, 3):
                fetches[i].wait()
            for ch in range(2):
                for j in range(2):
                    at_row = (2 * ch + j) * side
                    probe[at_row : at_row + side, :] = probe_in[ch, :, j * LANES : (j + 1) * LANES]

            halo_on(step)
            for i in (0, 1):
                fetches[i].wait()

            @pl.loop(0, positions)
            def _(p):
                a, b = lax.div(p, pos_cols), lax.rem(p, pos_cols)
                amp[p] = jnp.sqrt(jnp.maximum(patterns[a, b] - background[...], 0.0))
                edge = jnp.zeros((3, margin, LANES), F32)
                for lo in (0, wide):
                    lpad[p, :, lo : lo + margin, :] = edge
                    for ch in range(2):
                        pad[p, ch, :, lo : lo + margin, :] = edge

        chunk = 32

        @pl.loop(0, side // chunk)
        def _(i):
            r = i * chunk
            light = []
            for j in range(2):
                pr = probe[pl.ds(pl.multiple_of(j * side + r, chunk), chunk), :]
                pi = probe[pl.ds(pl.multiple_of((2 + j) * side + r, chunk), chunk), :]
                light.append(pr * pr + pi * pi)
            for p in range(positions):
                for j, part in enumerate(spread_lanes(light[0], light[1], starts(p)[1])):
                    lpad[p, j, pl.ds(pl.multiple_of(margin + r, chunk), chunk), :] = part

        def gather(source, to, s):
            row_starts = [starts(p)[0] for p in range(positions)]

            @pl.loop(0, margin // 64)
            def _(i):
                r = s * margin + i * 64
                for j in range(3):
                    parts = [source(p, j, pl.ds(margin - row_starts[p] + r, 64)) for p in range(positions)]
                    acc[to, j, pl.ds(pl.multiple_of(r, 64), 64), :] = functools.reduce(
                        lambda x, y: x + y, parts
                    )

            rs = pl.ds(s * margin, margin)
            k = sems["fold_col"] + 6 * to + 2 * s
            send(acc.at[to, 2, rs], got_col.at[0, to, rs], k, at(row, after), has_right)
            send(acc.at[to, 0, rs], got_col.at[1, to, rs], k + 1, at(row, before), has_left)

        def fold_cols(ch, s):
            rs = slice(s * margin, (s + 1) * margin)
            k = sems["fold_col"] + 6 * ch + 2 * s
            for side_at, cond in ((0, has_left), (1, has_right)):
                arrive(got_col.at[side_at, ch, rs], k + side_at, cond)

                @pl.when(cond)
                def _():
                    acc[ch, 1, rs] += got_col[side_at, ch, rs]

        def fold_rows(ch):
            k = sems["fold_row"] + 2 * ch
            fold_cols(ch, 0)
            send(acc.at[ch, 1, 0:margin], got_row.at[1, ch], k + 1, at(up, col), has_up)
            fold_cols(ch, 2)
            send(acc.at[ch, 1, 2 * margin : wide], got_row.at[0, ch], k, at(down, col), has_down)

        def fold_end(ch):
            k = sems["fold_row"] + 2 * ch
            fold_cols(ch, 1)
            for side_at, cond in ((0, has_up), (1, has_down)):
                arrive(got_row.at[side_at, ch], k + side_at, cond)

                @pl.when(cond)
                def _():
                    acc[ch, 1, margin : 2 * margin] += got_row[side_at, ch]

        for s in (0, 2, 1):
            gather(lambda p, j, rs: lpad[p, j, rs, :], 2, s)

        if step == 0:
            fetches[5].wait()
            real, imag = tables[0].astype(BF16), tables[1].astype(BF16)
            less = (-tables[1]).astype(BF16)
            for to, (one, two, three, four) in (
                (left, (real, less, imag, real)),
                (right, (real, imag, less, real)),
            ):
                to[0:side, 0:side] = one
                to[0:side, side : 2 * side] = two
                to[side : 2 * side, 0:side] = three
                to[side : 2 * side, side : 2 * side] = four
        halo_end(step)
        fold_rows(2)

        def probe_part(ch, j, r):
            at_row = (2 * ch + j) * side + r
            return probe[at_row : at_row + chunk, :]

        def leave(p, q):
            r0, c0 = starts(p)
            inside = lane_index(chunk) < LANES - c0
            turn = lax.rem(2 * LANES - c0, LANES)
            for r in range(0, side, chunk):
                parts = []
                for ch in range(2):
                    b = [
                        pltpu.roll(wide_ref[ch, j, pl.ds(r0 + r, chunk), :], turn, 1)
                        for j in range(3)
                    ]
                    parts.append([jnp.where(inside, b[j], b[j + 1]) for j in range(2)])
                for j in range(2):
                    wr, wi = parts[0][j], parts[1][j]
                    pr, pi = probe_part(0, j, r), probe_part(1, j, r)
                    lanes = slice(j * LANES, (j + 1) * LANES)
                    win[q, 0, r : r + chunk, lanes] = wr
                    win[q, 1, r : r + chunk, lanes] = wi
                    exit_b[q, r : r + chunk, lanes] = (pr * wr - pi * wi).astype(BF16)
                    exit_b[q, side + r : side + r + chunk, lanes] = (pr * wi + pi * wr).astype(BF16)

        def transform(one, two, q):
            halfway = jnp.dot(one[...], exit_b[q], preferred_element_type=F32).astype(BF16)
            half_b[q, :, 0:side] = halfway[0:side]
            half_b[q, :, side : 2 * side] = halfway[side : 2 * side]
            far[q] = jnp.dot(half_b[q], two[...], preferred_element_type=F32)

        def project(p, q):
            for r in range(0, side, chunk):
                fr, fi = far[q, r : r + chunk, 0:side], far[q, r : r + chunk, side : 2 * side]
                scale = amp[p, r : r + chunk, :] * lax.rsqrt(jnp.maximum(fr * fr + fi * fi, 0.25))
                exit_b[q, r : r + chunk, :] = (fr * scale).astype(BF16)
                exit_b[q, side + r : side + r + chunk, :] = (fi * scale).astype(BF16)

        def collect(places):
            for r in range(0, side, chunk):
                rs = slice(r, r + chunk)
                terms = [[[], []] for _ in places]
                for j in range(2):
                    lanes = slice(j * LANES, (j + 1) * LANES)
                    pr, pi = probe_part(0, j, r), probe_part(1, j, r)
                    sums = [0.0, 0.0]
                    for p, q in places:
                        wr, wi = win[q, 0, rs, lanes], win[q, 1, rs, lanes]
                        dr = far[q, rs, lanes] - (pr * wr - pi * wi)
                        di = far[q, rs, side + j * LANES : side + (j + 1) * LANES]
                        di = di - (pr * wi + pi * wr)
                        terms[q][0].append(pr * dr + pi * di)
                        terms[q][1].append(pr * di - pi * dr)
                        sums[0] += wr * dr + wi * di
                        sums[1] += wr * di - wi * dr
                    for ch in range(2):
                        at_row = (2 * ch + j) * side + r
                        grad[at_row : at_row + chunk, :] = sums[ch]
                for p, q in places:
                    c0 = starts(p)[1]
                    for ch in range(2):
                        for j, part in enumerate(spread_lanes(terms[q][ch][0], terms[q][ch][1], c0)):
                            pad[p, ch, j, margin + r : margin + r + chunk, :] = part

        places = [(p, p) for p in range(positions)]
        for p, q in places:
            leave(p, q)
        for p, q in places:
            transform(left, right, q)
            project(p, q)
        for p, q in places:
            transform(right, left, q)
        collect(places)

        def span(start, size):
            return pl.ds(pl.multiple_of(start, 8), size)

        mine, theirs = parity * half, (1 - parity) * half
        base_row = mine + row * by_row
        base_own = base_row + group * by_pair
        owns = None if owners == pairs else group < owners

        send(grad.at[span(theirs, half)], got_pair, sems["pair"], at(row, mate))
        for ch, s in ((0, 0), (0, 2), (1, 0), (1, 2), (0, 1), (1, 1)):
            gather(lambda p, j, rs, ch=ch: pad[p, ch, j, rs, :], ch, s)
        arrive(got_pair, sems["pair"])
        grad[span(mine, half), :] += got_pair[...]

        for d in range(1, rows):
            piece = grad.at[span(mine + row_pos(d) * by_row, by_row)]
            send(piece, got_rows.at[d - 1], sems["row_sum"] + d - 1, at(row_pos(d), col))
        fold_rows(0)
        for d in range(1, rows):
            arrive(got_rows.at[d - 1], sems["row_sum"] + d - 1)
        summed = grad[span(base_row, by_row), :]
        for d in range(1, rows):
            summed += got_rows[d - 1]
        grad[span(base_row, by_row), :] = summed

        for d in range(1, pairs):
            to = pair_pos(d)
            cond = None if owners == pairs else to < owners
            piece = grad.at[span(base_row + lax.min(to, owners - 1) * by_pair, by_pair)]
            send(piece, got_cols.at[d - 1], sems["col_sum"] + d - 1, at(row, 2 * to + parity), cond)
        fold_rows(1)
        for d in range(1, pairs):
            arrive(got_cols.at[d - 1], sems["col_sum"] + d - 1, owns)

        def finish():
            own = grad[span(base_own, by_pair), :]
            for d in range(1, pairs):
                own += got_cols[d - 1]
            total[span(base_own, by_pair), :] = own

        when(owns, finish)

        for d in range(1, pairs):
            piece = total.at[span(base_row + lax.min(group, owners - 1) * by_pair, by_pair)]
            device = at(row, 2 * pair_pos(d) + parity)
            send(piece, piece, sems["col_all"] + d - 1, device, owns)

        middle = slice(margin, 2 * margin)
        fold_end(2)
        for ch in range(2):
            fold_end(ch)
            changed = wide_ref[ch, 1, middle] + acc[ch, 1, middle] / (acc[2, 1, middle] + 1.0)
            if last:
                tile_end[ch] = changed
            else:
                per_iter[step + 1][0][ch, 1, middle] = changed
        if last:
            leaving = pltpu.make_async_copy(tile_end, tile_out, out_sem.at[0])
            leaving.start()
        else:
            halo_out(step + 1)

        for d in range(1, pairs):
            origin = pair_pos(pairs - d)
            cond = None if owners == pairs else origin < owners
            piece = total.at[span(base_row + lax.min(origin, owners - 1) * by_pair, by_pair)]
            arrive(piece, sems["col_all"] + d - 1, cond)
        piece = total.at[span(base_row, by_row)]
        for d in range(1, rows):
            send(piece, piece, sems["row_all"] + d - 1, at(row_pos(d), col))
        send(piece, piece, sems["pair_all"], at(row, mate))
        for d in range(1, rows):
            piece = total.at[span(mine + row_pos(rows - d) * by_row, by_row)]
            arrive(piece, sems["row_all"] + d - 1)
            send(piece, piece, sems["pair_all"] + d, at(row, mate))
        if not last:
            halo_on(step + 1)
        for d in range(rows):
            piece = total.at[span(theirs + row_pos(rows - d) * by_row, by_row)]
            arrive(piece, sems["pair_all"] + d)

        squares = jnp.zeros((8, LANES), F32)
        for i in range(4 * side // LANES):
            one = total[i * LANES : (i + 1) * LANES, :]
            squares += jnp.sum((one * one).reshape(LANES // 8, 8, LANES), axis=0)
        mean = jnp.sum(squares, keepdims=True) / (4 * side * LANES)
        scale = lax.rsqrt(mean + 1e-06)
        for ch in range(2):
            for j in range(2):
                at_row = (2 * ch + j) * side
                changed = probe[at_row : at_row + side, :] + total[at_row : at_row + side, :] * scale
                if last:
                    probe_end[ch, :, j * LANES : (j + 1) * LANES] = changed
                else:
                    probe[at_row : at_row + side, :] = changed

    parting = pltpu.make_async_copy(probe_end, probe_out, out_sem.at[1])
    parting.start()
    for cond, moved in started:
        when(cond, moved.wait_send)
    leaving.wait()
    parting.wait()


def hand_over(tile_in, probe_in, tile_out, probe_out, sem):
    moves = [
        pltpu.make_async_copy(tile_in, tile_out, sem.at[0]),
        pltpu.make_async_copy(probe_in, probe_out, sem.at[1]),
    ]
    for move in moves:
        move.start()
    for move in moves:
        move.wait()


def on_device(rows, cols, patterns, background, offsets, probe_wave, object_field):
    side = probe_wave.shape[-1]
    margin = side // 2
    wide = 3 * margin
    pos_rows, pos_cols = patterns.shape[0], patterns.shape[1]
    positions = pos_rows * pos_cols
    assert object_field.shape[1:] == (margin, LANES) and margin == LANES
    assert side == 2 * LANES and pos_rows * STEP == margin and pos_cols * STEP == LANES
    half, pairs, by_row, by_pair, _, _, count = plan(rows, cols, side)
    tables = dft_parts(side)
    scratch = [
        pltpu.VMEM((positions, side, side), F32),
        pltpu.VMEM((positions, 2, 3, wide + margin, LANES), F32),
        pltpu.VMEM((positions, 3, wide + margin, LANES), F32),
        pltpu.VMEM((positions, 2, side, side), F32),
        pltpu.VMEM((positions, 2 * side, side), BF16),
        pltpu.VMEM((positions, side, 2 * side), BF16),
        pltpu.VMEM((positions, side, 2 * side), F32),
        pltpu.VMEM((4 * side, LANES), F32),
        pltpu.VMEM(patterns.shape, F32),
        pltpu.VMEM(background.shape, F32),
        pltpu.SMEM(offsets.shape, jnp.int32),
        pltpu.VMEM(probe_wave.shape, F32),
        pltpu.VMEM(tables.shape, F32),
        pltpu.VMEM((2 * side, 2 * side), BF16),
        pltpu.VMEM((2 * side, 2 * side), BF16),
        pltpu.SemaphoreType.DMA((6,)),
        pltpu.VMEM(object_field.shape, F32),
        pltpu.VMEM(probe_wave.shape, F32),
        pltpu.SemaphoreType.DMA((2,)),
    ]
    for _ in range(ITERS):
        scratch += [
            pltpu.VMEM((2, 3, wide, LANES), F32),
            pltpu.VMEM((3, 3, wide, LANES), F32),
            pltpu.VMEM((2, 3, wide, LANES), F32),
            pltpu.VMEM((2, 3, margin, LANES), F32),
            pltpu.VMEM((4 * side, LANES), F32),
            pltpu.VMEM((half, LANES), F32),
            pltpu.VMEM((rows - 1, by_row, LANES), F32),
            pltpu.VMEM((pairs - 1, by_pair, LANES), F32),
            pltpu.VMEM((4 * side, LANES), F32),
            pltpu.SemaphoreType.DMA((count,)),
            pltpu.SemaphoreType.DMA((count,)),
        ]
    in_hbm = pl.BlockSpec(memory_space=pltpu.HBM)
    shapes = (
        jax.ShapeDtypeStruct(object_field.shape, F32),
        jax.ShapeDtypeStruct(probe_wave.shape, F32),
    )
    limit = 60 * 1024 * 1024
    tile, probe = pl.pallas_call(
        functools.partial(kernel, rows, cols, pos_rows, pos_cols, side),
        out_shape=shapes,
        in_specs=[in_hbm] * 6,
        out_specs=(in_hbm, in_hbm),
        scratch_shapes=scratch,
        compiler_params=pltpu.CompilerParams(
            collective_id=0, has_side_effects=True, vmem_limit_bytes=limit
        ),
    )(patterns, background, offsets, probe_wave, object_field, jnp.asarray(tables))
    return pl.pallas_call(
        hand_over,
        out_shape=shapes,
        in_specs=[in_hbm] * 2,
        out_specs=(in_hbm, in_hbm),
        scratch_shapes=[pltpu.SemaphoreType.DMA((2,))],
        compiler_params=pltpu.CompilerParams(vmem_limit_bytes=limit),
    )(tile, probe)


def solution(mesh):
    placed = (P("row", "col", None, None), P(), P("row", "col", None), P(), P(None, "row", "col"))
    return jax.shard_map(
        functools.partial(on_device, mesh.shape["row"], mesh.shape["col"]),
        mesh=mesh,
        in_specs=placed,
        out_specs=(P(None, "row", "col"), P()),
        check_vma=False,
    )
```

```python
import functools
import math

import jax
import jax.numpy as jnp
import numpy as np
from jax import lax
from jax.experimental import pallas as pl
from jax.experimental.pallas import tpu as pltpu
from jax.sharding import PartitionSpec as P

STEP = 64
ITERS = 2
LANES = 128
F32 = jnp.float32
BF16 = jnp.bfloat16


def dft_parts(side_len):
    indices = np.arange(side_len, dtype=np.int32)
    phases = indices[:, None] * indices[None, :] % side_len
    angles = phases.astype(np.float32) * np.float32(2.0 * math.pi / side_len)
    scaling = np.float32(1.0 / math.sqrt(side_len))
    real = (np.cos(angles) * scaling).astype(jnp.bfloat16)
    imag = (-np.sin(angles) * scaling).astype(jnp.bfloat16)
    return np.stack([real, imag]).astype(np.float32)


def plan(rows, cols, side):
    half = 2 * side
    pairs = cols // 2
    by_row = half // rows
    by_pair = max(8, by_row // pairs)
    owners = by_row // by_pair
    sems = {"halo": 0, "fold_col": 8, "fold_row": 26, "pair": 32}
    sems["row_sum"] = 33
    sems["col_sum"] = sems["row_sum"] + rows - 1
    sems["col_all"] = sems["col_sum"] + pairs - 1
    sems["row_all"] = sems["col_all"] + pairs - 1
    sems["pair_all"] = sems["row_all"] + rows - 1
    count = sems["pair_all"] + rows
    return half, pairs, by_row, by_pair, owners, sems, count


def kernel(rows, cols, pos_rows, pos_cols, side, *refs):
    inputs, (tile_out, probe_out) = refs[:6], refs[6:8]
    (amp, pad, lpad, win, exit_b, half_b, far, probe) = refs[8:16]
    (patterns, background, offsets, probe_in, tables, left, right, in_sem) = refs[16:24]
    (tile_end, probe_end, out_sem) = refs[24:27]
    per_iter = [refs[27 + 11 * i : 38 + 11 * i] for i in range(ITERS)]
    half, pairs, by_row, by_pair, owners, sems, _ = plan(rows, cols, side)
    margin = side // 2
    wide = 3 * margin
    positions = pos_rows * pos_cols
    row, col = lax.axis_index("row"), lax.axis_index("col")
    parity = lax.rem(col, 2)
    mate = col + 1 - 2 * parity
    group = lax.div(col, 2)
    has_up, has_down = row > 0, row < rows - 1
    has_left, has_right = col > 0, col < cols - 1
    up, down = lax.max(row - 1, 0), lax.min(row + 1, rows - 1)
    before, after = lax.max(col - 1, 0), lax.min(col + 1, cols - 1)
    started = [[] for _ in range(ITERS)]

    def at(r, c):
        return {"row": r, "col": c}

    def when(cond, act):
        if cond is None:
            act()
        else:
            pl.when(cond)(act)

    def row_pos(d):
        return lax.rem(row + d, rows)

    def pair_pos(d):
        return lax.rem(group + d, pairs)

    barrier = pltpu.get_barrier_semaphore()

    def greet(device):
        pl.semaphore_signal(barrier, inc=1, device_id=device, device_id_type=pl.DeviceIdType.MESH)

    for d in range(1, rows):
        greet(at(row_pos(d), col))
    for d in range(1, pairs):
        greet(at(row, 2 * pair_pos(d) + parity))
    when(has_left, lambda: greet(at(row, before)))
    when(has_right, lambda: greet(at(row, after)))

    def lane_index(n):
        return lax.broadcasted_iota(jnp.int32, (n, LANES), 1)

    def starts(p):
        a, b = lax.div(p, pos_cols), lax.rem(p, pos_cols)
        return a * STEP + offsets[a, b, 0], b * STEP + offsets[a, b, 1]

    def spread_lanes(first, second, c0):
        keep = lane_index(first.shape[0]) >= c0
        turn = lax.rem(c0, LANES)
        first, second = pltpu.roll(first, turn, 1), pltpu.roll(second, turn, 1)
        zero = jnp.zeros_like(first)
        return (
            jnp.where(keep, first, zero),
            jnp.where(keep, second, first),
            jnp.where(keep, zero, second),
        )

    centre = per_iter[0][0].at[:, 1, margin : 2 * margin, :]
    homes = (patterns, background, offsets, probe_in, centre, tables)
    fetches = [pltpu.make_async_copy(a, b, in_sem.at[i]) for i, (a, b) in enumerate(zip(inputs, homes))]
    for i in (4, 3, 2, 0, 1, 5):
        fetches[i].start()
    for wide_ref in (it[0] for it in per_iter):
        zeros = jnp.zeros((2, 3, margin, LANES), F32)

        @pl.when(row == 0)
        def _():
            wide_ref[:, :, 0:margin, :] = zeros

        @pl.when(row == rows - 1)
        def _():
            wide_ref[:, :, 2 * margin : wide, :] = zeros

        @pl.when(col == 0)
        def _():
            wide_ref[:, 0] = jnp.zeros((2, wide, LANES), F32)

        @pl.when(col == cols - 1)
        def _():
            wide_ref[:, 2] = jnp.zeros((2, wide, LANES), F32)

    beside = lax.min(col, 1) + lax.min(cols - 1 - col, 1)
    fetches[4].wait()
    pl.semaphore_wait(barrier, rows - 1 + pairs - 1 + beside)

    def link(step):
        s_sem, r_sem = per_iter[step][9:11]

        def copy(src, dst, k, device):
            return pltpu.make_async_remote_copy(
                src_ref=src,
                dst_ref=dst,
                send_sem=s_sem.at[k],
                recv_sem=r_sem.at[k],
                device_id=device,
                device_id_type=pl.DeviceIdType.MESH,
            )

        def send(src, dst, k, device, cond=None):
            moved = copy(src, dst, k, device)
            when(cond, moved.start)
            started[step].append((cond, moved))

        def arrive(dst, k, cond=None):
            when(cond, copy(dst, dst, k, at(row, mate)).wait_recv)

        return send, arrive

    def drain(step, leave=0):
        ready = len(started[step]) - leave
        for cond, moved in started[step][:ready]:
            when(cond, moved.wait_send)
        del started[step][:ready]

    def thirds(step):
        return lambda j, s: per_iter[step][0].at[:, j, s * margin : (s + 1) * margin, :]

    def strip_on(step, s, cond):
        send, third = link(step)[0], thirds(step)
        base = sems["halo"] + 2 + s
        go_right = has_right if cond is None else jnp.logical_and(has_right, cond)
        go_left = has_left if cond is None else jnp.logical_and(has_left, cond)
        send(third(1, s), third(0, s), base, at(row, after), go_right)
        send(third(1, s), third(2, s), base + 3, at(row, before), go_left)

    def halo_out(step):
        send, third = link(step)[0], thirds(step)
        send(third(1, 1), third(1, 0), sems["halo"], at(down, col), has_down)
        send(third(1, 1), third(1, 2), sems["halo"] + 1, at(up, col), has_up)
        strip_on(step, 1, None)

    def halo_on(step):
        arrive, third = link(step)[1], thirds(step)
        arrive(third(1, 0), sems["halo"], has_up)
        strip_on(step, 0, has_up)
        arrive(third(1, 2), sems["halo"] + 1, has_down)
        strip_on(step, 2, has_down)

    def halo_end(step):
        arrive, third = link(step)[1], thirds(step)
        for s, cond in ((1, None), (0, has_up), (2, has_down)):
            base = sems["halo"] + 2 + s
            from_left = has_left if cond is None else jnp.logical_and(has_left, cond)
            from_right = has_right if cond is None else jnp.logical_and(has_right, cond)
            arrive(third(0, s), base, from_left)
            arrive(third(2, s), base + 3, from_right)

    for step in range(ITERS):
        wide_ref, acc, got_col, got_row, grad, got_pair, got_rows, got_cols, total, s_sem, r_sem = (
            per_iter[step]
        )
        last = step == ITERS - 1

        send, arrive = link(step)
        third = thirds(step)
        if step == 0:
            halo_out(step)

        if step == 0:
            for i in (2, 3):
                fetches[i].wait()
            for ch in range(2):
                for j in range(2):
                    at_row = (2 * ch + j) * side
                    probe[at_row : at_row + side, :] = probe_in[ch, :, j * LANES : (j + 1) * LANES]

            for i in (0, 1):
                fetches[i].wait()

            @pl.loop(0, positions)
            def _(p):
                a, b = lax.div(p, pos_cols), lax.rem(p, pos_cols)
                amp[p] = jnp.sqrt(jnp.maximum(patterns[a, b] - background[...], 0.0))
                edge = jnp.zeros((3, margin, LANES), F32)
                for lo in (0, wide):
                    lpad[p, :, lo : lo + margin, :] = edge
                    for ch in range(2):
                        pad[p, ch, :, lo : lo + margin, :] = edge

            fetches[5].wait()
            real, imag = tables[0].astype(BF16), tables[1].astype(BF16)
            less = (-tables[1]).astype(BF16)
            for to, (one, two, three, four) in (
                (left, (real, less, imag, real)),
                (right, (real, imag, less, real)),
            ):
                to[0:side, 0:side] = one
                to[0:side, side : 2 * side] = two
                to[side : 2 * side, 0:side] = three
                to[side : 2 * side, side : 2 * side] = four

        chunk = 32

        @pl.loop(0, side // chunk)
        def _(i):
            r = i * chunk
            light = []
            for j in range(2):
                pr = probe[pl.ds(pl.multiple_of(j * side + r, chunk), chunk), :]
                pi = probe[pl.ds(pl.multiple_of((2 + j) * side + r, chunk), chunk), :]
                light.append(pr * pr + pi * pi)
            for p in range(positions):
                for j, part in enumerate(spread_lanes(light[0], light[1], starts(p)[1])):
                    lpad[p, j, pl.ds(pl.multiple_of(margin + r, chunk), chunk), :] = part

        def gather(source, to, s):
            row_starts = [starts(p)[0] for p in range(positions)]

            @pl.loop(0, margin // 64)
            def _(i):
                r = s * margin + i * 64
                for j in range(3):
                    parts = [source(p, j, pl.ds(margin - row_starts[p] + r, 64)) for p in range(positions)]
                    acc[to, j, pl.ds(pl.multiple_of(r, 64), 64), :] = functools.reduce(
                        lambda x, y: x + y, parts
                    )

            rs = pl.ds(s * margin, margin)
            k = sems["fold_col"] + 6 * to + 2 * s
            send(acc.at[to, 2, rs], got_col.at[0, to, rs], k, at(row, after), has_right)
            send(acc.at[to, 0, rs], got_col.at[1, to, rs], k + 1, at(row, before), has_left)

        def fold_cols(ch, s):
            rs = slice(s * margin, (s + 1) * margin)
            k = sems["fold_col"] + 6 * ch + 2 * s
            for side_at, cond in ((0, has_left), (1, has_right)):
                arrive(got_col.at[side_at, ch, rs], k + side_at, cond)

                @pl.when(cond)
                def _():
                    acc[ch, 1, rs] += got_col[side_at, ch, rs]

        def fold_rows(ch):
            k = sems["fold_row"] + 2 * ch
            fold_cols(ch, 0)
            send(acc.at[ch, 1, 0:margin], got_row.at[1, ch], k + 1, at(up, col), has_up)
            fold_cols(ch, 2)
            send(acc.at[ch, 1, 2 * margin : wide], got_row.at[0, ch], k, at(down, col), has_down)

        def fold_end(ch):
            k = sems["fold_row"] + 2 * ch
            fold_cols(ch, 1)
            for side_at, cond in ((0, has_up), (1, has_down)):
                arrive(got_row.at[side_at, ch], k + side_at, cond)

                @pl.when(cond)
                def _():
                    acc[ch, 1, margin : 2 * margin] += got_row[side_at, ch]

        if step == 0:
            halo_on(step)
        for s in (0, 2, 1):
            gather(lambda p, j, rs: lpad[p, j, rs, :], 2, s)

        if step > 0:
            drain(step - 1)
        halo_end(step)

        def probe_part(ch, j, r):
            at_row = (2 * ch + j) * side + r
            return probe[at_row : at_row + chunk, :]

        def leave(p, q):
            r0, c0 = starts(p)
            inside = lane_index(chunk) < LANES - c0
            turn = lax.rem(2 * LANES - c0, LANES)
            for r in range(0, side, chunk):
                parts = []
                for ch in range(2):
                    b = [
                        pltpu.roll(wide_ref[ch, j, pl.ds(r0 + r, chunk), :], turn, 1)
                        for j in range(3)
                    ]
                    parts.append([jnp.where(inside, b[j], b[j + 1]) for j in range(2)])
                for j in range(2):
                    wr, wi = parts[0][j], parts[1][j]
                    pr, pi = probe_part(0, j, r), probe_part(1, j, r)
                    lanes = slice(j * LANES, (j + 1) * LANES)
                    win[q, 0, r : r + chunk, lanes] = wr
                    win[q, 1, r : r + chunk, lanes] = wi
                    exit_b[q, r : r + chunk, lanes] = (pr * wr - pi * wi).astype(BF16)
                    exit_b[q, side + r : side + r + chunk, lanes] = (pr * wi + pi * wr).astype(BF16)

        def transform(one, two, q):
            halfway = jnp.dot(one[...], exit_b[q], preferred_element_type=F32).astype(BF16)
            half_b[q, :, 0:side] = halfway[0:side]
            half_b[q, :, side : 2 * side] = halfway[side : 2 * side]
            far[q] = jnp.dot(half_b[q], two[...], preferred_element_type=F32)

        def project(p, q):
            for r in range(0, side, chunk):
                fr, fi = far[q, r : r + chunk, 0:side], far[q, r : r + chunk, side : 2 * side]
                scale = amp[p, r : r + chunk, :] * lax.rsqrt(jnp.maximum(fr * fr + fi * fi, 0.25))
                exit_b[q, r : r + chunk, :] = (fr * scale).astype(BF16)
                exit_b[q, side + r : side + r + chunk, :] = (fi * scale).astype(BF16)

        def collect(places):
            for r in range(0, side, chunk):
                rs = slice(r, r + chunk)
                terms = [[[], []] for _ in places]
                for j in range(2):
                    lanes = slice(j * LANES, (j + 1) * LANES)
                    pr, pi = probe_part(0, j, r), probe_part(1, j, r)
                    sums = [0.0, 0.0]
                    for p, q in places:
                        wr, wi = win[q, 0, rs, lanes], win[q, 1, rs, lanes]
                        dr = far[q, rs, lanes] - (pr * wr - pi * wi)
                        di = far[q, rs, side + j * LANES : side + (j + 1) * LANES]
                        di = di - (pr * wi + pi * wr)
                        terms[q][0].append(pr * dr + pi * di)
                        terms[q][1].append(pr * di - pi * dr)
                        sums[0] += wr * dr + wi * di
                        sums[1] += wr * di - wi * dr
                    for ch in range(2):
                        at_row = (2 * ch + j) * side + r
                        grad[at_row : at_row + chunk, :] = sums[ch]
                for p, q in places:
                    c0 = starts(p)[1]
                    for ch in range(2):
                        for j, part in enumerate(spread_lanes(terms[q][ch][0], terms[q][ch][1], c0)):
                            pad[p, ch, j, margin + r : margin + r + chunk, :] = part

        places = [(p, p) for p in range(positions)]
        for p, q in places:
            leave(p, q)
        for p, q in places:
            transform(left, right, q)
            project(p, q)
        fold_rows(2)
        for p, q in places:
            transform(right, left, q)
        collect(places)

        def span(start, size):
            return pl.ds(pl.multiple_of(start, 8), size)

        mine, theirs = parity * half, (1 - parity) * half
        base_row = mine + row * by_row
        base_own = base_row + group * by_pair
        owns = None if owners == pairs else group < owners

        send(grad.at[span(theirs, half)], got_pair, sems["pair"], at(row, mate))
        for ch, s in ((0, 0), (0, 2), (1, 0), (1, 2), (0, 1), (1, 1)):
            gather(lambda p, j, rs, ch=ch: pad[p, ch, j, rs, :], ch, s)
        arrive(got_pair, sems["pair"])
        grad[span(mine, half), :] += got_pair[...]

        for d in range(1, rows):
            piece = grad.at[span(mine + row_pos(d) * by_row, by_row)]
            send(piece, got_rows.at[d - 1], sems["row_sum"] + d - 1, at(row_pos(d), col))
        fold_rows(0)
        for d in range(1, rows):
            arrive(got_rows.at[d - 1], sems["row_sum"] + d - 1)
        summed = grad[span(base_row, by_row), :]
        for d in range(1, rows):
            summed += got_rows[d - 1]
        grad[span(base_row, by_row), :] = summed

        for d in range(1, pairs):
            to = pair_pos(d)
            cond = None if owners == pairs else to < owners
            piece = grad.at[span(base_row + lax.min(to, owners - 1) * by_pair, by_pair)]
            send(piece, got_cols.at[d - 1], sems["col_sum"] + d - 1, at(row, 2 * to + parity), cond)
        fold_rows(1)
        for d in range(1, pairs):
            arrive(got_cols.at[d - 1], sems["col_sum"] + d - 1, owns)

        def finish():
            own = grad[span(base_own, by_pair), :]
            for d in range(1, pairs):
                own += got_cols[d - 1]
            total[span(base_own, by_pair), :] = own

        when(owns, finish)

        for d in range(1, pairs):
            piece = total.at[span(base_row + lax.min(group, owners - 1) * by_pair, by_pair)]
            device = at(row, 2 * pair_pos(d) + parity)
            send(piece, piece, sems["col_all"] + d - 1, device, owns)

        middle = slice(margin, 2 * margin)
        fold_end(2)
        for ch in range(2):
            fold_end(ch)
            changed = wide_ref[ch, 1, middle] + acc[ch, 1, middle] / (acc[2, 1, middle] + 1.0)
            if last:
                tile_end[ch] = changed
            else:
                per_iter[step + 1][0][ch, 1, middle] = changed
        if last:
            leaving = pltpu.make_async_copy(tile_end, tile_out, out_sem.at[0])
            leaving.start()
        else:
            halo_out(step + 1)

        for d in range(1, pairs):
            origin = pair_pos(pairs - d)
            cond = None if owners == pairs else origin < owners
            piece = total.at[span(base_row + lax.min(origin, owners - 1) * by_pair, by_pair)]
            arrive(piece, sems["col_all"] + d - 1, cond)
        piece = total.at[span(base_row, by_row)]
        for d in range(1, rows):
            send(piece, piece, sems["row_all"] + d - 1, at(row_pos(d), col))
        send(piece, piece, sems["pair_all"], at(row, mate))
        for d in range(1, rows):
            piece = total.at[span(mine + row_pos(rows - d) * by_row, by_row)]
            arrive(piece, sems["row_all"] + d - 1)
            send(piece, piece, sems["pair_all"] + d, at(row, mate))
        if not last:
            halo_on(step + 1)
        if last:
            drain(step, rows)
        for d in range(rows):
            piece = total.at[span(theirs + row_pos(rows - d) * by_row, by_row)]
            arrive(piece, sems["pair_all"] + d)

        squares = jnp.zeros((8, LANES), F32)
        for i in range(4 * side // LANES):
            one = total[i * LANES : (i + 1) * LANES, :]
            squares += jnp.sum((one * one).reshape(LANES // 8, 8, LANES), axis=0)
        mean = jnp.sum(squares, keepdims=True) / (4 * side * LANES)
        scale = lax.rsqrt(mean + 1e-06)
        for ch in range(2):
            for j in range(2):
                at_row = (2 * ch + j) * side
                changed = probe[at_row : at_row + side, :] + total[at_row : at_row + side, :] * scale
                if last:
                    probe_end[ch, :, j * LANES : (j + 1) * LANES] = changed
                else:
                    probe[at_row : at_row + side, :] = changed

    parting = pltpu.make_async_copy(probe_end, probe_out, out_sem.at[1])
    parting.start()
    drain(ITERS - 1)
    leaving.wait()
    parting.wait()


def hand_over(tile_in, probe_in, tile_out, probe_out, tile, probe, sem):
    entering = [
        pltpu.make_async_copy(probe_in, probe, sem.at[0]),
        pltpu.make_async_copy(tile_in, tile, sem.at[1]),
    ]
    leaving = [
        pltpu.make_async_copy(probe, probe_out, sem.at[2]),
        pltpu.make_async_copy(tile, tile_out, sem.at[3]),
    ]
    for move in entering:
        move.start()
    for move, onward in zip(entering, leaving):
        move.wait()
        onward.start()
    for move in leaving:
        move.wait()


def on_device(rows, cols, patterns, background, offsets, probe_wave, object_field):
    side = probe_wave.shape[-1]
    margin = side // 2
    wide = 3 * margin
    pos_rows, pos_cols = patterns.shape[0], patterns.shape[1]
    positions = pos_rows * pos_cols
    assert object_field.shape[1:] == (margin, LANES) and margin == LANES
    assert side == 2 * LANES and pos_rows * STEP == margin and pos_cols * STEP == LANES
    half, pairs, by_row, by_pair, _, _, count = plan(rows, cols, side)
    tables = dft_parts(side)
    scratch = [
        pltpu.VMEM((positions, side, side), F32),
        pltpu.VMEM((positions, 2, 3, wide + margin, LANES), F32),
        pltpu.VMEM((positions, 3, wide + margin, LANES), F32),
        pltpu.VMEM((positions, 2, side, side), F32),
        pltpu.VMEM((positions, 2 * side, side), BF16),
        pltpu.VMEM((positions, side, 2 * side), BF16),
        pltpu.VMEM((positions, side, 2 * side), F32),
        pltpu.VMEM((4 * side, LANES), F32),
        pltpu.VMEM(patterns.shape, F32),
        pltpu.VMEM(background.shape, F32),
        pltpu.SMEM(offsets.shape, jnp.int32),
        pltpu.VMEM(probe_wave.shape, F32),
        pltpu.VMEM(tables.shape, F32),
        pltpu.VMEM((2 * side, 2 * side), BF16),
        pltpu.VMEM((2 * side, 2 * side), BF16),
        pltpu.SemaphoreType.DMA((6,)),
        pltpu.VMEM(object_field.shape, F32),
        pltpu.VMEM(probe_wave.shape, F32),
        pltpu.SemaphoreType.DMA((2,)),
    ]
    for _ in range(ITERS):
        scratch += [
            pltpu.VMEM((2, 3, wide, LANES), F32),
            pltpu.VMEM((3, 3, wide, LANES), F32),
            pltpu.VMEM((2, 3, wide, LANES), F32),
            pltpu.VMEM((2, 3, margin, LANES), F32),
            pltpu.VMEM((4 * side, LANES), F32),
            pltpu.VMEM((half, LANES), F32),
            pltpu.VMEM((rows - 1, by_row, LANES), F32),
            pltpu.VMEM((pairs - 1, by_pair, LANES), F32),
            pltpu.VMEM((4 * side, LANES), F32),
            pltpu.SemaphoreType.DMA((count,)),
            pltpu.SemaphoreType.DMA((count,)),
        ]
    in_hbm = pl.BlockSpec(memory_space=pltpu.HBM)
    shapes = (
        jax.ShapeDtypeStruct(object_field.shape, F32),
        jax.ShapeDtypeStruct(probe_wave.shape, F32),
    )
    limit = 60 * 1024 * 1024
    tile, probe = pl.pallas_call(
        functools.partial(kernel, rows, cols, pos_rows, pos_cols, side),
        out_shape=shapes,
        in_specs=[in_hbm] * 6,
        out_specs=(in_hbm, in_hbm),
        scratch_shapes=scratch,
        compiler_params=pltpu.CompilerParams(
            collective_id=0, has_side_effects=True, vmem_limit_bytes=limit
        ),
    )(patterns, background, offsets, probe_wave, object_field, jnp.asarray(tables))
    return pl.pallas_call(
        hand_over,
        out_shape=shapes,
        in_specs=[in_hbm] * 2,
        out_specs=(in_hbm, in_hbm),
        scratch_shapes=[
            pltpu.VMEM(object_field.shape, F32),
            pltpu.VMEM(probe_wave.shape, F32),
            pltpu.SemaphoreType.DMA((4,)),
        ],
        compiler_params=pltpu.CompilerParams(vmem_limit_bytes=limit),
    )(tile, probe)


def solution(mesh):
    placed = (P("row", "col", None, None), P(), P("row", "col", None), P(), P(None, "row", "col"))
    return jax.shard_map(
        functools.partial(on_device, mesh.shape["row"], mesh.shape["col"]),
        mesh=mesh,
        in_specs=placed,
        out_specs=(P(None, "row", "col"), P()),
        check_vma=False,
    )
```

```python
import functools
import math

import jax
import jax.numpy as jnp
import numpy as np
from jax import lax
from jax.experimental import pallas as pl
from jax.experimental.pallas import tpu as pltpu
from jax.sharding import PartitionSpec as P

STEP = 64
ITERS = 2
LANES = 128
F32 = jnp.float32
BF16 = jnp.bfloat16


def dft_parts(side_len):
    indices = np.arange(side_len, dtype=np.int32)
    phases = indices[:, None] * indices[None, :] % side_len
    angles = phases.astype(np.float32) * np.float32(2.0 * math.pi / side_len)
    scaling = np.float32(1.0 / math.sqrt(side_len))
    real = (np.cos(angles) * scaling).astype(jnp.bfloat16)
    imag = (-np.sin(angles) * scaling).astype(jnp.bfloat16)
    return np.stack([real, imag]).astype(np.float32)


def plan(rows, cols, side):
    half = 2 * side
    pairs = cols // 2
    by_row = half // rows
    by_pair = max(8, by_row // pairs)
    owners = by_row // by_pair
    sems = {"halo": 0, "fold_col": 8, "fold_row": 26, "pair": 32}
    sems["row_sum"] = 33
    sems["col_sum"] = sems["row_sum"] + rows - 1
    sems["col_all"] = sems["col_sum"] + pairs - 1
    sems["row_all"] = sems["col_all"] + pairs - 1
    sems["pair_all"] = sems["row_all"] + rows - 1
    count = sems["pair_all"] + rows
    return half, pairs, by_row, by_pair, owners, sems, count


def kernel(rows, cols, pos_rows, pos_cols, side, *refs):
    inputs, (tile_out, probe_out) = refs[:6], refs[6:8]
    (amp, pad, lpad, win, exit_b, half_b, far, probe) = refs[8:16]
    (patterns, background, offsets, probe_in, tables, left, right, in_sem) = refs[16:24]
    (tile_end, probe_end, out_sem) = refs[24:27]
    per_iter = [refs[27 + 11 * i : 38 + 11 * i] for i in range(ITERS)]
    half, pairs, by_row, by_pair, owners, sems, _ = plan(rows, cols, side)
    margin = side // 2
    wide = 3 * margin
    positions = pos_rows * pos_cols
    row, col = lax.axis_index("row"), lax.axis_index("col")
    parity = lax.rem(col, 2)
    mate = col + 1 - 2 * parity
    group = lax.div(col, 2)
    has_up, has_down = row > 0, row < rows - 1
    has_left, has_right = col > 0, col < cols - 1
    up, down = lax.max(row - 1, 0), lax.min(row + 1, rows - 1)
    before, after = lax.max(col - 1, 0), lax.min(col + 1, cols - 1)
    started = [[] for _ in range(ITERS)]

    def at(r, c):
        return {"row": r, "col": c}

    def when(cond, act):
        if cond is None:
            act()
        else:
            pl.when(cond)(act)

    def row_pos(d):
        return lax.rem(row + d, rows)

    def pair_pos(d):
        return lax.rem(group + d, pairs)

    barrier = pltpu.get_barrier_semaphore()

    def greet(device):
        pl.semaphore_signal(barrier, inc=1, device_id=device, device_id_type=pl.DeviceIdType.MESH)

    for d in range(1, rows):
        greet(at(row_pos(d), col))
    for d in range(1, pairs):
        greet(at(row, 2 * pair_pos(d) + parity))
    when(has_left, lambda: greet(at(row, before)))
    when(has_right, lambda: greet(at(row, after)))

    def lane_index(n):
        return lax.broadcasted_iota(jnp.int32, (n, LANES), 1)

    def starts(p):
        a, b = lax.div(p, pos_cols), lax.rem(p, pos_cols)
        return a * STEP + offsets[a, b, 0], b * STEP + offsets[a, b, 1]

    def spread_lanes(first, second, c0):
        keep = lane_index(first.shape[0]) >= c0
        turn = lax.rem(c0, LANES)
        first, second = pltpu.roll(first, turn, 1), pltpu.roll(second, turn, 1)
        zero = jnp.zeros_like(first)
        return (
            jnp.where(keep, first, zero),
            jnp.where(keep, second, first),
            jnp.where(keep, zero, second),
        )

    centre = per_iter[0][0].at[:, 1, margin : 2 * margin, :]
    homes = (patterns, background, offsets, probe_in, centre, tables)
    fetches = [pltpu.make_async_copy(a, b, in_sem.at[i]) for i, (a, b) in enumerate(zip(inputs, homes))]
    for i in (4, 3, 2, 0, 1, 5):
        fetches[i].start()
    for wide_ref in (it[0] for it in per_iter):
        zeros = jnp.zeros((2, 3, margin, LANES), F32)

        @pl.when(row == 0)
        def _():
            wide_ref[:, :, 0:margin, :] = zeros

        @pl.when(row == rows - 1)
        def _():
            wide_ref[:, :, 2 * margin : wide, :] = zeros

        @pl.when(col == 0)
        def _():
            wide_ref[:, 0] = jnp.zeros((2, wide, LANES), F32)

        @pl.when(col == cols - 1)
        def _():
            wide_ref[:, 2] = jnp.zeros((2, wide, LANES), F32)

    beside = lax.min(col, 1) + lax.min(cols - 1 - col, 1)
    fetches[4].wait()
    pl.semaphore_wait(barrier, rows - 1 + pairs - 1 + beside)

    def link(step):
        s_sem, r_sem = per_iter[step][9:11]

        def copy(src, dst, k, device):
            return pltpu.make_async_remote_copy(
                src_ref=src,
                dst_ref=dst,
                send_sem=s_sem.at[k],
                recv_sem=r_sem.at[k],
                device_id=device,
                device_id_type=pl.DeviceIdType.MESH,
            )

        def send(src, dst, k, device, cond=None):
            moved = copy(src, dst, k, device)
            when(cond, moved.start)
            started[step].append((cond, moved))

        def arrive(dst, k, cond=None):
            when(cond, copy(dst, dst, k, at(row, mate)).wait_recv)

        return send, arrive

    def drain(step, leave=0):
        ready = len(started[step]) - leave
        for cond, moved in started[step][:ready]:
            when(cond, moved.wait_send)
        del started[step][:ready]

    def thirds(step):
        return lambda j, s: per_iter[step][0].at[:, j, s * margin : (s + 1) * margin, :]

    def strip_on(step, s, cond):
        send, third = link(step)[0], thirds(step)
        base = sems["halo"] + 2 + s
        go_right = has_right if cond is None else jnp.logical_and(has_right, cond)
        go_left = has_left if cond is None else jnp.logical_and(has_left, cond)
        send(third(1, s), third(0, s), base, at(row, after), go_right)
        send(third(1, s), third(2, s), base + 3, at(row, before), go_left)

    def halo_out(step):
        send, third = link(step)[0], thirds(step)
        send(third(1, 1), third(1, 0), sems["halo"], at(down, col), has_down)
        send(third(1, 1), third(1, 2), sems["halo"] + 1, at(up, col), has_up)
        strip_on(step, 1, None)

    def halo_on(step):
        arrive, third = link(step)[1], thirds(step)
        arrive(third(1, 0), sems["halo"], has_up)
        strip_on(step, 0, has_up)
        arrive(third(1, 2), sems["halo"] + 1, has_down)
        strip_on(step, 2, has_down)

    def halo_end(step):
        arrive, third = link(step)[1], thirds(step)
        for s, cond in ((1, None), (0, has_up), (2, has_down)):
            base = sems["halo"] + 2 + s
            from_left = has_left if cond is None else jnp.logical_and(has_left, cond)
            from_right = has_right if cond is None else jnp.logical_and(has_right, cond)
            arrive(third(0, s), base, from_left)
            arrive(third(2, s), base + 3, from_right)

    for step in range(ITERS):
        wide_ref, acc, got_col, got_row, grad, got_pair, got_rows, got_cols, total, s_sem, r_sem = (
            per_iter[step]
        )
        last = step == ITERS - 1

        send, arrive = link(step)
        third = thirds(step)
        if step == 0:
            halo_out(step)

        if step == 0:
            for i in (2, 3):
                fetches[i].wait()
            for ch in range(2):
                for j in range(2):
                    at_row = (2 * ch + j) * side
                    probe[at_row : at_row + side, :] = probe_in[ch, :, j * LANES : (j + 1) * LANES]

            for i in (0, 1):
                fetches[i].wait()

            @pl.loop(0, positions)
            def _(p):
                a, b = lax.div(p, pos_cols), lax.rem(p, pos_cols)
                amp[p] = jnp.sqrt(jnp.maximum(patterns[a, b] - background[...], 0.0))
                edge = jnp.zeros((3, margin, LANES), F32)
                for lo in (0, wide):
                    lpad[p, :, lo : lo + margin, :] = edge
                    for ch in range(2):
                        pad[p, ch, :, lo : lo + margin, :] = edge

            fetches[5].wait()
            real, imag = tables[0].astype(BF16), tables[1].astype(BF16)
            less = (-tables[1]).astype(BF16)
            for to, (one, two, three, four) in (
                (left, (real, less, imag, real)),
                (right, (real, imag, less, real)),
            ):
                to[0:side, 0:side] = one
                to[0:side, side : 2 * side] = two
                to[side : 2 * side, 0:side] = three
                to[side : 2 * side, side : 2 * side] = four

        chunk = 32

        @pl.loop(0, side // chunk)
        def _(i):
            r = i * chunk
            light = []
            for j in range(2):
                pr = probe[pl.ds(pl.multiple_of(j * side + r, chunk), chunk), :]
                pi = probe[pl.ds(pl.multiple_of((2 + j) * side + r, chunk), chunk), :]
                light.append(pr * pr + pi * pi)
            for p in range(positions):
                for j, part in enumerate(spread_lanes(light[0], light[1], starts(p)[1])):
                    lpad[p, j, pl.ds(pl.multiple_of(margin + r, chunk), chunk), :] = part

        def gather(source, to, s):
            row_starts = [starts(p)[0] for p in range(positions)]

            @pl.loop(0, margin // 64)
            def _(i):
                r = s * margin + i * 64
                for j in range(3):
                    parts = [source(p, j, pl.ds(margin - row_starts[p] + r, 64)) for p in range(positions)]
                    acc[to, j, pl.ds(pl.multiple_of(r, 64), 64), :] = functools.reduce(
                        lambda x, y: x + y, parts
                    )

            rs = pl.ds(s * margin, margin)
            k = sems["fold_col"] + 6 * to + 2 * s
            send(acc.at[to, 2, rs], got_col.at[0, to, rs], k, at(row, after), has_right)
            send(acc.at[to, 0, rs], got_col.at[1, to, rs], k + 1, at(row, before), has_left)

        def fold_cols(ch, s):
            rs = slice(s * margin, (s + 1) * margin)
            k = sems["fold_col"] + 6 * ch + 2 * s
            for side_at, cond in ((0, has_left), (1, has_right)):
                arrive(got_col.at[side_at, ch, rs], k + side_at, cond)

                @pl.when(cond)
                def _():
                    acc[ch, 1, rs] += got_col[side_at, ch, rs]

        def fold_rows(ch):
            k = sems["fold_row"] + 2 * ch
            fold_cols(ch, 0)
            send(acc.at[ch, 1, 0:margin], got_row.at[1, ch], k + 1, at(up, col), has_up)
            fold_cols(ch, 2)
            send(acc.at[ch, 1, 2 * margin : wide], got_row.at[0, ch], k, at(down, col), has_down)

        def fold_end(ch):
            k = sems["fold_row"] + 2 * ch
            fold_cols(ch, 1)
            for side_at, cond in ((0, has_up), (1, has_down)):
                arrive(got_row.at[side_at, ch], k + side_at, cond)

                @pl.when(cond)
                def _():
                    acc[ch, 1, margin : 2 * margin] += got_row[side_at, ch]

        if step == 0:
            halo_on(step)
        for s in (0, 2, 1):
            gather(lambda p, j, rs: lpad[p, j, rs, :], 2, s)

        if step > 0:
            drain(step - 1)
        halo_end(step)

        def probe_part(ch, j, r):
            at_row = (2 * ch + j) * side + r
            return probe[at_row : at_row + chunk, :]

        def leave(p, q):
            r0, c0 = starts(p)
            inside = lane_index(chunk) < LANES - c0
            turn = lax.rem(2 * LANES - c0, LANES)
            for r in range(0, side, chunk):
                parts = []
                for ch in range(2):
                    b = [
                        pltpu.roll(wide_ref[ch, j, pl.ds(r0 + r, chunk), :], turn, 1)
                        for j in range(3)
                    ]
                    parts.append([jnp.where(inside, b[j], b[j + 1]) for j in range(2)])
                for j in range(2):
                    wr, wi = parts[0][j], parts[1][j]
                    pr, pi = probe_part(0, j, r), probe_part(1, j, r)
                    lanes = slice(j * LANES, (j + 1) * LANES)
                    win[q, 0, r : r + chunk, lanes] = wr
                    win[q, 1, r : r + chunk, lanes] = wi
                    exit_b[q, r : r + chunk, lanes] = (pr * wr - pi * wi).astype(BF16)
                    exit_b[q, side + r : side + r + chunk, lanes] = (pr * wi + pi * wr).astype(BF16)

        def transform(one, two, q):
            halfway = jnp.dot(one[...], exit_b[q], preferred_element_type=F32).astype(BF16)
            half_b[q, :, 0:side] = halfway[0:side]
            half_b[q, :, side : 2 * side] = halfway[side : 2 * side]
            far[q] = jnp.dot(half_b[q], two[...], preferred_element_type=F32)

        def project(p, q):
            for r in range(0, side, chunk):
                fr, fi = far[q, r : r + chunk, 0:side], far[q, r : r + chunk, side : 2 * side]
                scale = amp[p, r : r + chunk, :] * lax.rsqrt(jnp.maximum(fr * fr + fi * fi, 0.25))
                exit_b[q, r : r + chunk, :] = (fr * scale).astype(BF16)
                exit_b[q, side + r : side + r + chunk, :] = (fi * scale).astype(BF16)

        def collect(places):
            for r in range(0, side, chunk):
                rs = slice(r, r + chunk)
                terms = [[[], []] for _ in places]
                for j in range(2):
                    lanes = slice(j * LANES, (j + 1) * LANES)
                    pr, pi = probe_part(0, j, r), probe_part(1, j, r)
                    sums = [0.0, 0.0]
                    for p, q in places:
                        wr, wi = win[q, 0, rs, lanes], win[q, 1, rs, lanes]
                        dr = far[q, rs, lanes] - (pr * wr - pi * wi)
                        di = far[q, rs, side + j * LANES : side + (j + 1) * LANES]
                        di = di - (pr * wi + pi * wr)
                        terms[q][0].append(pr * dr + pi * di)
                        terms[q][1].append(pr * di - pi * dr)
                        sums[0] += wr * dr + wi * di
                        sums[1] += wr * di - wi * dr
                    for ch in range(2):
                        at_row = (2 * ch + j) * side + r
                        grad[at_row : at_row + chunk, :] = sums[ch]
                for p, q in places:
                    c0 = starts(p)[1]
                    for ch in range(2):
                        for j, part in enumerate(spread_lanes(terms[q][ch][0], terms[q][ch][1], c0)):
                            pad[p, ch, j, margin + r : margin + r + chunk, :] = part

        places = [(p, p) for p in range(positions)]
        for p, q in places:
            leave(p, q)
        for p, q in places:
            transform(left, right, q)
            project(p, q)
        fold_rows(2)
        for p, q in places:
            transform(right, left, q)
        collect(places)

        def span(start, size):
            return pl.ds(pl.multiple_of(start, 8), size)

        mine, theirs = parity * half, (1 - parity) * half
        base_row = mine + row * by_row
        base_own = base_row + group * by_pair
        owns = None if owners == pairs else group < owners

        send(grad.at[span(theirs, half)], got_pair, sems["pair"], at(row, mate))
        for ch, s in ((0, 0), (0, 2), (1, 0), (1, 2)):
            gather(lambda p, j, rs, ch=ch: pad[p, ch, j, rs, :], ch, s)
        arrive(got_pair, sems["pair"])
        grad[span(mine, half), :] += got_pair[...]

        for d in range(1, rows):
            piece = grad.at[span(mine + row_pos(d) * by_row, by_row)]
            send(piece, got_rows.at[d - 1], sems["row_sum"] + d - 1, at(row_pos(d), col))
        for ch in range(2):
            gather(lambda p, j, rs, ch=ch: pad[p, ch, j, rs, :], ch, 1)
        fold_rows(0)
        for d in range(1, rows):
            arrive(got_rows.at[d - 1], sems["row_sum"] + d - 1)
        summed = grad[span(base_row, by_row), :]
        for d in range(1, rows):
            summed += got_rows[d - 1]
        grad[span(base_row, by_row), :] = summed

        for d in range(1, pairs):
            to = pair_pos(d)
            cond = None if owners == pairs else to < owners
            piece = grad.at[span(base_row + lax.min(to, owners - 1) * by_pair, by_pair)]
            send(piece, got_cols.at[d - 1], sems["col_sum"] + d - 1, at(row, 2 * to + parity), cond)
        fold_rows(1)
        for d in range(1, pairs):
            arrive(got_cols.at[d - 1], sems["col_sum"] + d - 1, owns)

        def finish():
            own = grad[span(base_own, by_pair), :]
            for d in range(1, pairs):
                own += got_cols[d - 1]
            total[span(base_own, by_pair), :] = own

        when(owns, finish)

        for d in range(1, pairs):
            piece = total.at[span(base_row + lax.min(group, owners - 1) * by_pair, by_pair)]
            device = at(row, 2 * pair_pos(d) + parity)
            send(piece, piece, sems["col_all"] + d - 1, device, owns)

        middle = slice(margin, 2 * margin)
        fold_end(2)
        for ch in range(2):
            fold_end(ch)
            changed = wide_ref[ch, 1, middle] + acc[ch, 1, middle] / (acc[2, 1, middle] + 1.0)
            if last:
                tile_end[ch] = changed
            else:
                per_iter[step + 1][0][ch, 1, middle] = changed
        if last:
            leaving = pltpu.make_async_copy(tile_end, tile_out, out_sem.at[0])
            leaving.start()
        else:
            halo_out(step + 1)

        for d in range(1, pairs):
            origin = pair_pos(pairs - d)
            cond = None if owners == pairs else origin < owners
            piece = total.at[span(base_row + lax.min(origin, owners - 1) * by_pair, by_pair)]
            arrive(piece, sems["col_all"] + d - 1, cond)
        piece = total.at[span(base_row, by_row)]
        for d in range(1, rows):
            send(piece, piece, sems["row_all"] + d - 1, at(row_pos(d), col))
        send(piece, piece, sems["pair_all"], at(row, mate))
        for d in range(1, rows):
            piece = total.at[span(mine + row_pos(rows - d) * by_row, by_row)]
            arrive(piece, sems["row_all"] + d - 1)
            send(piece, piece, sems["pair_all"] + d, at(row, mate))
        if not last:
            halo_on(step + 1)
        if last:
            drain(step, rows)
        for d in range(rows):
            piece = total.at[span(theirs + row_pos(rows - d) * by_row, by_row)]
            arrive(piece, sems["pair_all"] + d)

        squares = jnp.zeros((8, LANES), F32)
        for i in range(4 * side // LANES):
            one = total[i * LANES : (i + 1) * LANES, :]
            squares += jnp.sum((one * one).reshape(LANES // 8, 8, LANES), axis=0)
        mean = jnp.sum(squares, keepdims=True) / (4 * side * LANES)
        scale = lax.rsqrt(mean + 1e-06)
        for ch in range(2):
            for j in range(2):
                at_row = (2 * ch + j) * side
                changed = probe[at_row : at_row + side, :] + total[at_row : at_row + side, :] * scale
                if last:
                    probe_end[ch, :, j * LANES : (j + 1) * LANES] = changed
                else:
                    probe[at_row : at_row + side, :] = changed

    parting = pltpu.make_async_copy(probe_end, probe_out, out_sem.at[1])
    parting.start()
    drain(ITERS - 1)
    leaving.wait()
    parting.wait()


def hand_over(tile_in, probe_in, tile_out, probe_out, tile, probe, sem):
    entering = [
        pltpu.make_async_copy(probe_in, probe, sem.at[0]),
        pltpu.make_async_copy(tile_in, tile, sem.at[1]),
    ]
    leaving = [
        pltpu.make_async_copy(probe, probe_out, sem.at[2]),
        pltpu.make_async_copy(tile, tile_out, sem.at[3]),
    ]
    for move in entering:
        move.start()
    for move, onward in zip(entering, leaving):
        move.wait()
        onward.start()
    for move in leaving:
        move.wait()


def on_device(rows, cols, patterns, background, offsets, probe_wave, object_field):
    side = probe_wave.shape[-1]
    margin = side // 2
    wide = 3 * margin
    pos_rows, pos_cols = patterns.shape[0], patterns.shape[1]
    positions = pos_rows * pos_cols
    assert object_field.shape[1:] == (margin, LANES) and margin == LANES
    assert side == 2 * LANES and pos_rows * STEP == margin and pos_cols * STEP == LANES
    half, pairs, by_row, by_pair, _, _, count = plan(rows, cols, side)
    tables = dft_parts(side)
    scratch = [
        pltpu.VMEM((positions, side, side), F32),
        pltpu.VMEM((positions, 2, 3, wide + margin, LANES), F32),
        pltpu.VMEM((positions, 3, wide + margin, LANES), F32),
        pltpu.VMEM((positions, 2, side, side), F32),
        pltpu.VMEM((positions, 2 * side, side), BF16),
        pltpu.VMEM((positions, side, 2 * side), BF16),
        pltpu.VMEM((positions, side, 2 * side), F32),
        pltpu.VMEM((4 * side, LANES), F32),
        pltpu.VMEM(patterns.shape, F32),
        pltpu.VMEM(background.shape, F32),
        pltpu.SMEM(offsets.shape, jnp.int32),
        pltpu.VMEM(probe_wave.shape, F32),
        pltpu.VMEM(tables.shape, F32),
        pltpu.VMEM((2 * side, 2 * side), BF16),
        pltpu.VMEM((2 * side, 2 * side), BF16),
        pltpu.SemaphoreType.DMA((6,)),
        pltpu.VMEM(object_field.shape, F32),
        pltpu.VMEM(probe_wave.shape, F32),
        pltpu.SemaphoreType.DMA((2,)),
    ]
    for _ in range(ITERS):
        scratch += [
            pltpu.VMEM((2, 3, wide, LANES), F32),
            pltpu.VMEM((3, 3, wide, LANES), F32),
            pltpu.VMEM((2, 3, wide, LANES), F32),
            pltpu.VMEM((2, 3, margin, LANES), F32),
            pltpu.VMEM((4 * side, LANES), F32),
            pltpu.VMEM((half, LANES), F32),
            pltpu.VMEM((rows - 1, by_row, LANES), F32),
            pltpu.VMEM((pairs - 1, by_pair, LANES), F32),
            pltpu.VMEM((4 * side, LANES), F32),
            pltpu.SemaphoreType.DMA((count,)),
            pltpu.SemaphoreType.DMA((count,)),
        ]
    in_hbm = pl.BlockSpec(memory_space=pltpu.HBM)
    shapes = (
        jax.ShapeDtypeStruct(object_field.shape, F32),
        jax.ShapeDtypeStruct(probe_wave.shape, F32),
    )
    limit = 60 * 1024 * 1024
    tile, probe = pl.pallas_call(
        functools.partial(kernel, rows, cols, pos_rows, pos_cols, side),
        out_shape=shapes,
        in_specs=[in_hbm] * 6,
        out_specs=(in_hbm, in_hbm),
        scratch_shapes=scratch,
        compiler_params=pltpu.CompilerParams(
            collective_id=0, has_side_effects=True, vmem_limit_bytes=limit
        ),
    )(patterns, background, offsets, probe_wave, object_field, jnp.asarray(tables))
    return pl.pallas_call(
        hand_over,
        out_shape=shapes,
        in_specs=[in_hbm] * 2,
        out_specs=(in_hbm, in_hbm),
        scratch_shapes=[
            pltpu.VMEM(object_field.shape, F32),
            pltpu.VMEM(probe_wave.shape, F32),
            pltpu.SemaphoreType.DMA((4,)),
        ],
        compiler_params=pltpu.CompilerParams(vmem_limit_bytes=limit),
    )(tile, probe)


def solution(mesh):
    placed = (P("row", "col", None, None), P(), P("row", "col", None), P(), P(None, "row", "col"))
    return jax.shard_map(
        functools.partial(on_device, mesh.shape["row"], mesh.shape["col"]),
        mesh=mesh,
        in_specs=placed,
        out_specs=(P(None, "row", "col"), P()),
        check_vma=False,
    )
```
